256 devices in a mesh: dp: 32 (over y_hi, z, core), tensor: 8 (over x, y_lo).
Axes of the slice: x: 4, y: 4 (y_hi: 2, y_lo: 2; y = y_hi * 2 + y_lo), z: 8, core: 2. Of those that a mesh axis runs over, the one named last changes fastest.
Arguments:
- checkpoint: bfloat16 [12288, 8192], P(('dp', 'tensor')), may hold values from -400 to 400
- gain: bfloat16 [8192], replicated, may hold values from 0.099609375 to 1.8984375
- qkv_weight: bfloat16 [8192, 5120], P(None, 'tensor'), may hold values from -0.0625 to 0.0625
- qkv_cot: bfloat16 [12288, 5120], P('dp', 'tensor'), may hold values from -6 to 6
Outputs:
- input_grad: bfloat16 [12288, 8192], P(('dp', 'tensor'))
- gain_grad: float32 [8192], P('dp')
- qkv_weight_grad: float32 [8192, 5120], P('dp', 'tensor')
The draws below stay inside these ranges and needn't reach their ends.
All inputs are finite; a program needn't handle non-finite values.
Results may differ from the reference program's by a relative error of at most 0.019.
Values may be sent and summed in bfloat16 or wider, within the bound.
No kernel may reach another device: no remote copies, remote signals or barrier semaphores. Data moves between devices by JAX's collectives and lax.ppermute only.
A program may use at most 128 MiB of HBM per device.

```python
import math
import jax
import jax.numpy as jnp
from jax import lax

D = 8192
TOK = 384
QKV = 5120
TOKENS = 12288
N_DP = 32
N_TENSOR = 8


def draw_checkpoint(key, part):
    key = jax.random.fold_in(key, 11)
    first, second, third = jax.random.split(key, 3)
    base = jnp.clip(jax.random.normal(first, (TOKENS, D), jnp.float32), -4.0, 4.0)
    row_top = math.log(10.0)
    col_top = math.log(10.0)
    row_scale = jnp.exp(jax.random.uniform(second, (TOKENS, 1), jnp.float32, 0.0, row_top))
    col_scale = jnp.exp(jax.random.uniform(third, (1, D), jnp.float32, 0.0, col_top))
    return (base * row_scale * col_scale).astype(jnp.bfloat16)


def block_scale(key, extent, shards, low, high):
    level, own = 1.0, jax.random.fold_in(key, 6)
    for axis_at, parts in shards:
        steps = jnp.exp(jax.random.uniform(jax.random.fold_in(own, axis_at), (parts,), jnp.float32, low / len(shards), high / len(shards)))
        level = level * jnp.repeat(steps, extent[axis_at] // parts).reshape([-1 if axis == axis_at else 1 for axis in range(len(extent))])
    return level


def scatter_about(stream_key, extent, deviation, bound, pieces=(), kind=jnp.bfloat16):
    values = deviation * jax.random.normal(stream_key, extent, jnp.float32)
    if pieces:
        values = values * block_scale(stream_key, extent, pieces, -0.22, 0.18)
    return jnp.clip(values, -bound, bound).astype(kind)


def setup_inputs(seed: int = 0) -> dict:
    key_list = jax.random.split(jax.random.key(seed), 5)
    return {
        "checkpoint": draw_checkpoint(jax.random.fold_in(key_list[4], 71), 0),
        "gain": jnp.clip(1.0 + 0.18 * jax.random.normal(key_list[1], (D,), jnp.float32), 0.099609375, 1.8984375).astype(jnp.bfloat16),
        "qkv_weight": scatter_about(key_list[2], (D, QKV), D ** -0.5, 0.0625, ((1, 8),)),
        "qkv_cot": scatter_about(key_list[3], (TOKENS, QKV), 1.0, 6.0, ((0, 32), (1, 8))),
    }


def reference(checkpoint, gain, qkv_weight, qkv_cot):
    rows = checkpoint.astype(jnp.float32)
    inv_rms = lax.rsqrt(lax.optimization_barrier(jnp.mean(rows * rows, axis=1, keepdims=True)) + 1e-05)
    unit_rows = rows * inv_rms
    gain_f = gain.astype(jnp.float32)
    normed = (unit_rows * gain_f).astype(jnp.bfloat16)
    grad_scale = 1.0 / math.sqrt(TOKENS)
    weight_total = jnp.zeros((D, QKV), jnp.float32)
    for group in range(N_DP):
        lower = group * TOK
        upper = lower + TOK
        term = lax.dot_general(normed[lower:upper], qkv_cot[lower:upper], (((0,), (0,)), ((), ())), preferred_element_type=jnp.float32) * grad_scale
        rounded = lax.optimization_barrier(term.astype(jnp.bfloat16))
        weight_total = weight_total + rounded.astype(jnp.float32)
    group_cols = QKV // N_TENSOR
    normed_grad = jnp.zeros((TOKENS, D), jnp.float32)
    for group in range(N_TENSOR):
        lower = group * group_cols
        upper = lower + group_cols
        term = lax.dot_general(qkv_cot[:, lower:upper], qkv_weight[:, lower:upper], (((1,), (1,)), ((), ())), preferred_element_type=jnp.float32)
        partial_sum = lax.optimization_barrier(term.astype(jnp.bfloat16))
        normed_grad = normed_grad + partial_sum.astype(jnp.float32)
    gain_grad = lax.optimization_barrier(jnp.sum(normed_grad * unit_rows, axis=0)) * grad_scale
    scaled = normed_grad * gain_f
    input_grad = (inv_rms * (scaled - unit_rows * lax.optimization_barrier(jnp.mean(scaled * unit_rows, axis=1, keepdims=True)))).astype(jnp.bfloat16)
    return (input_grad, gain_grad, weight_total)
```

```python
import functools
import math

import jax
import jax.numpy as jnp
from jax import lax
from jax.experimental import pallas as pl
from jax.experimental.pallas import tpu as pltpu
from jax.sharding import Mesh
from jax.sharding import PartitionSpec as P

H, Z, C, X, L = 2, 8, 2, 4, 2
T = X * L
DP = ("h", "z", "c")
TENSOR = ("x", "l")
BF = jnp.bfloat16
F32 = jnp.float32


def shift(value, axis, step):
    n = lax.axis_size(axis)
    return lax.ppermute(value, axis, [(i, (i + step) % n) for i in range(n)])


def swap(value, axis):
    return shift(value, axis, 1)


def relative(blocks, x, l):
    turned = lax.dynamic_slice_in_dim(jnp.concatenate([blocks, blocks], 0), x, X, 0)
    return jnp.where(l == 0, turned, turned[:, ::-1])


def absolute(blocks, x, l):
    return relative(blocks, lax.rem(X - x, X), l)


def terms_kernel(cot_ref, w_ref, *outs):
    product = lax.dot_general(
        cot_ref[...], w_ref[...], (((1,), (1,)), ((), ())), preferred_element_type=F32
    ).astype(BF)
    rows = product.shape[0] // len(outs)
    for i, out in enumerate(outs):
        out[...] = product[i * rows : (i + 1) * rows]


def grad_terms(cot, weight, tile=512):
    rows, depth = cot.shape
    width = weight.shape[0]
    own = rows // T
    return pl.pallas_call(
        terms_kernel,
        grid=(width // tile,),
        in_specs=[
            pl.BlockSpec((rows, depth), lambda i: (0, 0)),
            pl.BlockSpec((tile, depth), lambda i: (i, 0)),
        ],
        out_specs=[pl.BlockSpec((own, tile), lambda i: (0, i))] * T,
        out_shape=[jax.ShapeDtypeStruct((own, width), BF)] * T,
        compiler_params=pltpu.CompilerParams(vmem_limit_bytes=32 << 20),
        cost_estimate=pl.CostEstimate(
            flops=2 * rows * depth * width,
            bytes_accessed=2 * (rows * depth + width * depth + rows * width),
            transcendentals=0,
        ),
    )(cot, weight)


def weight_kernel(scale, count, left_ref, *refs):
    out = refs[-1]
    left = left_ref[...]
    for i in range(count):
        right = jnp.concatenate([refs[i][...], refs[count + i][...]], axis=0)
        product = lax.dot_general(left, right, (((1,), (0,)), ((), ())), preferred_element_type=F32)
        product = (product * scale).astype(BF)
        out[:, i] = product.reshape(out.shape[0], *out.shape[2:])


def weight_terms(left, own, other, scale):
    features, tokens = left.shape
    columns = own[0].shape[1]
    count = len(own)
    return pl.pallas_call(
        functools.partial(weight_kernel, scale, count),
        in_specs=[pl.BlockSpec(memory_space=pltpu.VMEM)] * (1 + 2 * count),
        out_specs=pl.BlockSpec(memory_space=pltpu.VMEM),
        out_shape=jax.ShapeDtypeStruct((Z, count, features // Z, columns), BF),
        compiler_params=pltpu.CompilerParams(vmem_limit_bytes=40 << 20),
        cost_estimate=pl.CostEstimate(
            flops=2 * features * tokens * columns * count,
            bytes_accessed=2 * (features * tokens + (tokens + features) * columns * count),
            transcendentals=0,
        ),
    )(left, *own, *other)


def add(*values):
    total = values[0].astype(F32)
    for value in values[1:]:
        total = total + value.astype(F32)
    return total


def shards(checkpoint, gain, qkv_weight, qkv_cot):
    h, c = lax.axis_index("h"), lax.axis_index("c")
    x, l = lax.axis_index("x"), lax.axis_index("l")
    local, width = checkpoint.shape
    tokens, columns = qkv_cot.shape
    grad_scale = 1.0 / math.sqrt(tokens * H * Z * C)
    fine = width // (H * Z * C * T)
    gain_f = gain.astype(F32)

    with jax.named_scope("cot_gather"):
        near = {(0, 0): qkv_cot}
        near[0, 1] = swap(qkv_cot, "l")
        near[3, 0] = shift(qkv_cot, "x", 1)
        near[1, 0] = shift(qkv_cot, "x", -1)
        half = tokens // 2
        first = shift(near[3, 0][:half], "x", 1)
        second = shift(near[1, 0][half:], "x", -1)
        near[3, 1] = shift(near[0, 1], "x", 1)
        near[1, 1] = shift(near[0, 1], "x", -1)
        near[2, 0] = jnp.concatenate([first, second], 0)
        near[2, 1] = swap(near[2, 0], "l")
        across = {key: swap(value, "c") for key, value in near.items()}

    with jax.named_scope("normed_exchange"):
        rows = checkpoint.astype(F32)
        inv_rms = lax.rsqrt(jnp.mean(rows * rows, axis=1, keepdims=True) + 1e-05)
        unit_rows = rows * inv_rms
        normed = (unit_rows * gain_f).astype(BF)
        parts = normed.reshape(local, H, Z * C * T * fine)
        parts = jnp.where(h == 0, parts, parts[:, ::-1])
        parts = parts.reshape(local, H, Z, C, T, fine).transpose(3, 4, 0, 2, 1, 5)
        parts = parts.reshape(C * T * local, Z * H * fine)
        left = lax.all_to_all(parts, ("c",) + TENSOR, 0, 0, tiled=True)
        left = left.reshape(C, tokens, Z * H * fine)
        left = jnp.where(c == 0, left, left[::-1]).reshape(C * tokens, Z * H * fine).T

    with jax.named_scope("input_terms"):
        cot_near = relative(qkv_cot.reshape(X, L, local, columns), x, l)
        term = grad_terms(cot_near.reshape(tokens, columns), qkv_weight)
        term = {(i // L, i % L): term[i] for i in range(T)}
        far_up = shift(term[2, 0], "x", 1)
        far_down = shift(term[2, 1], "x", -1)
        up_1 = shift(term[1, 1], "x", 1)
        down_0 = shift(term[3, 0], "x", -1)
        up_0 = shift(add(term[1, 0], far_up).astype(BF), "x", 1)
        down_1 = shift(add(term[3, 1], far_down).astype(BF), "x", -1)
        other_l = swap(add(term[0, 1], up_1, down_1).astype(BF), "l")
        normed_grad = add(term[0, 0], up_0, down_0, other_l)

    with jax.named_scope("input_out"):
        gain_part = jnp.sum(normed_grad * unit_rows, axis=0) * grad_scale
        scaled = normed_grad * gain_f
        input_grad = (
            inv_rms * (scaled - unit_rows * jnp.mean(scaled * unit_rows, axis=1, keepdims=True))
        ).astype(BF)
        gain_out = lax.psum(
            lax.psum_scatter(gain_part, DP, scatter_dimension=0, tiled=True), TENSOR
        )

    with jax.named_scope("weight_terms"):
        sums = {}
        for keys in (((0, 0), (0, 1), (1, 0), (3, 0)), ((2, 0), (1, 1), (3, 1), (2, 1))):
            part = weight_terms(
                left, [near[k] for k in keys], [across[k] for k in keys], grad_scale
            )
            part = part.reshape(-1, columns)
            part = lax.psum_scatter(part, "z", scatter_dimension=0, tiled=True)
            part = part.reshape(len(keys), H, fine, columns)
            part = add(part[:, 0], swap(part[:, 1], "h")).astype(BF)
            for i, key in enumerate(keys):
                sums[key] = part[i]
    with jax.named_scope("weight_out"):
        blocks = jnp.stack([sums[i, j] for i in range(X) for j in range(L)])
        blocks = absolute(blocks.reshape(X, L, fine, columns), x, l).reshape(T * fine, columns)
        weight_out = lax.all_to_all(blocks, TENSOR, 0, 0, tiled=True).astype(F32)
    return (input_grad, gain_out, weight_out)


def solution(mesh):
    fine_mesh = Mesh(mesh.devices.reshape(H, Z, C, X, L), DP + TENSOR)
    rows = P(DP + TENSOR, None)
    in_specs = (rows, P(), P(None, TENSOR), P(DP, TENSOR))
    out_specs = (rows, P(DP), P(DP, TENSOR))
    return jax.shard_map(
        shards, mesh=fine_mesh, in_specs=in_specs, out_specs=out_specs, check_vma=False
    )
```

```python
import functools
import math

import jax
import jax.numpy as jnp
from jax import lax
from jax.experimental import pallas as pl
from jax.experimental.pallas import tpu as pltpu
from jax.sharding import Mesh
from jax.sharding import PartitionSpec as P

H, Z, C, X, L = 2, 8, 2, 4, 2
T = X * L
DP = ("h", "z", "c")
TENSOR = ("x", "l")
BF = jnp.bfloat16
F32 = jnp.float32


def shift(value, axis, step):
    n = lax.axis_size(axis)
    return lax.ppermute(value, axis, [(i, (i + step) % n) for i in range(n)])


def swap(value, axis):
    return shift(value, axis, 1)


def relative(blocks, x, l):
    turned = lax.dynamic_slice_in_dim(jnp.concatenate([blocks, blocks], 0), x, X, 0)
    return jnp.where(l == 0, turned, turned[:, ::-1])


def terms_kernel(cot_ref, w_ref, *outs):
    product = lax.dot_general(
        cot_ref[...], w_ref[...], (((1,), (1,)), ((), ())), preferred_element_type=F32
    ).astype(BF)
    rows = product.shape[0] // len(outs)
    for i, out in enumerate(outs):
        out[...] = product[i * rows : (i + 1) * rows]


def grad_terms(cot, weight, tile=512):
    rows, depth = cot.shape
    width = weight.shape[0]
    own = rows // T
    return pl.pallas_call(
        terms_kernel,
        grid=(width // tile,),
        in_specs=[
            pl.BlockSpec((rows, depth), lambda i: (0, 0)),
            pl.BlockSpec((tile, depth), lambda i: (i, 0)),
        ],
        out_specs=[pl.BlockSpec((own, tile), lambda i: (0, i))] * T,
        out_shape=[jax.ShapeDtypeStruct((own, width), BF)] * T,
        compiler_params=pltpu.CompilerParams(vmem_limit_bytes=32 << 20),
        cost_estimate=pl.CostEstimate(
            flops=2 * rows * depth * width,
            bytes_accessed=2 * (rows * depth + width * depth + rows * width),
            transcendentals=0,
        ),
    )(cot, weight)


def weight_kernel(scale, count, order_ref, left_ref, *refs):
    out = refs[-1]
    for i in range(count):

        @pl.when(pl.program_id(0) == i)
        def _():
            right = jnp.concatenate([refs[i][...], refs[count + i][...]], axis=0)
            product = lax.dot_general(
                left_ref[...], right, (((1,), (0,)), ((), ())), preferred_element_type=F32
            )
            out[...] = (product * scale).astype(BF).reshape(out.shape)


def weight_terms(order, left, own, other, scale, so_far=None):
    features, tokens = left.shape
    columns = own[0].shape[1]
    count = len(own)
    fine = features // (Z * H)
    whole = lambda shape: pl.BlockSpec(shape, lambda i, order: (0, 0))
    in_specs = [whole((features, tokens))] + [whole(own[0].shape)] * (2 * count)
    given = [] if so_far is None else [so_far]
    in_specs += [pl.BlockSpec(memory_space=pl.ANY)] * len(given)
    return pl.pallas_call(
        functools.partial(weight_kernel, scale, count),
        grid_spec=pltpu.PrefetchScalarGridSpec(
            num_scalar_prefetch=1,
            grid=(count,),
            in_specs=in_specs,
            out_specs=pl.BlockSpec(
                (Z, H, 1, fine, columns), lambda i, order: (0, 0, order[i], 0, 0)
            ),
        ),
        out_shape=jax.ShapeDtypeStruct((Z, H, T, fine, columns), BF),
        input_output_aliases={2 + 2 * count: 0} if given else {},
        compiler_params=pltpu.CompilerParams(vmem_limit_bytes=40 << 20),
        cost_estimate=pl.CostEstimate(
            flops=2 * features * tokens * columns * count,
            bytes_accessed=2 * (features * tokens + (tokens + features) * columns * count),
            transcendentals=0,
        ),
    )(order, left, *own, *other, *given)


def normed_kernel(check_ref, gain_ref, out_ref):
    local, width = check_ref.shape
    span = width // (H * Z * C)
    fine = span // T
    per = 128 // fine
    values = check_ref[...].astype(F32)
    inv_rms = lax.rsqrt(jnp.mean(values * values, axis=1, keepdims=True) + 1e-05)
    normed = (values * inv_rms * gain_ref[...].astype(F32)).astype(BF)
    groups = Z * H // per
    lines = []
    for c in range(C):
        for group in range(groups):
            pieces = []
            for k in range(per):
                z, h = divmod(group * per + k, H)
                at = ((h * Z + z) * C + c) * span
                pieces.append(normed[:, at : at + span])
            lines.append(jnp.concatenate(pieces, axis=1))
    stacked = jnp.concatenate(lines, axis=0)
    size = per * span
    row = lax.broadcasted_iota(jnp.int32, (size, size), 0)
    column = lax.broadcasted_iota(jnp.int32, (size, size), 1)
    k, t, i = row // span, (row // fine) % T, row % fine
    places = jnp.where(column == t * 128 + k * fine + i, 1.0, 0.0).astype(BF)
    placed = jnp.dot(stacked, places, preferred_element_type=F32).astype(BF)
    for c in range(C):
        for group in range(groups):
            at = (c * groups + group) * local
            for t in range(T):
                out_ref[c * T + t, :, group * 128 : (group + 1) * 128] = placed[
                    at : at + local, t * 128 : (t + 1) * 128
                ]


def normed_parts(checkpoint, gain):
    local, width = checkpoint.shape
    return pl.pallas_call(
        normed_kernel,
        in_specs=[pl.BlockSpec(memory_space=pltpu.VMEM)] * 2,
        out_specs=pl.BlockSpec(memory_space=pltpu.VMEM),
        out_shape=jax.ShapeDtypeStruct((C * T, local, width // (C * T)), BF),
        compiler_params=pltpu.CompilerParams(vmem_limit_bytes=40 << 20),
        cost_estimate=pl.CostEstimate(
            flops=2 * local * width * 1024, bytes_accessed=4 * local * width, transcendentals=0
        ),
    )(checkpoint, gain.reshape(1, width))


def after(values, *others):
    return lax.optimization_barrier((values, *others))[0]


def add(*values):
    total = values[0].astype(F32)
    for value in values[1:]:
        total = total + value.astype(F32)
    return total


def shards(checkpoint, gain, qkv_weight, qkv_cot):
    h, z, c = lax.axis_index("h"), lax.axis_index("z"), lax.axis_index("c")
    x, l = lax.axis_index("x"), lax.axis_index("l")
    local, width = checkpoint.shape
    tokens, columns = qkv_cot.shape
    grad_scale = 1.0 / math.sqrt(tokens * H * Z * C)
    fine = width // (H * Z * C * T)
    gain_f = gain.astype(F32)

    with jax.named_scope("cot_gather"):
        near = {(0, 0): qkv_cot}
        near[0, 1] = swap(qkv_cot, "l")
        for step in (1, 3, 2):
            near[step, 0] = shift(qkv_cot, "x", -step)
        near[3, 1] = shift(near[0, 1], "x", 1)
        near[1, 1] = shift(near[0, 1], "x", -1)
        near[2, 1] = swap(near[2, 0], "l")
        across = {key: swap(value, "c") for key, value in near.items()}

    with jax.named_scope("normed_exchange"):
        parts = normed_parts(checkpoint, gain)
        left = lax.all_to_all(parts, ("c",) + TENSOR, 0, 0, tiled=True)
        left = left.reshape(C, tokens, Z * H * fine)
        left = jnp.where(c == 0, left, left[::-1]).reshape(C * tokens, Z * H * fine).T

    with jax.named_scope("input_terms"):
        cot_near = relative(qkv_cot.reshape(X, L, local, columns), x, l)
        cot_near = after(cot_near.reshape(tokens, columns), parts, near[0, 1])
        term = grad_terms(cot_near, qkv_weight)
        term = after(term, near[1, 1], near[3, 1])
        term = {(i // L, i % L): term[i] for i in range(T)}

    with jax.named_scope("weight_terms"):
        part = None
        for keys in (((0, 0), (0, 1), (1, 0), (3, 0), (2, 0)), ((1, 1), (3, 1), (2, 1))):
            order = jnp.stack([lax.rem(x + i, X) * L + lax.rem(l + j, L) for i, j in keys])
            part = weight_terms(
                order if part is None else after(order, term[0, 0]), left, [near[k] for k in keys], [across[k] for k in keys], grad_scale, part
            )
        sums = lax.psum_scatter(part.reshape(-1, columns), "z", scatter_dimension=0, tiled=True)

    with jax.named_scope("input_sums"):
        far_up = shift(term[2, 0], "x", 1)
        far_down = shift(term[2, 1], "x", -1)
        up_1 = shift(term[1, 1], "x", 1)
        down_0 = shift(term[3, 0], "x", -1)
        next_up, next_down = after((term[1, 0], term[3, 1]), part)
        up_0 = shift(add(next_up, far_up).astype(BF), "x", 1)
        down_1 = shift(add(next_down, far_down).astype(BF), "x", -1)
        other_l = swap(add(term[0, 1], up_1, down_1).astype(BF), "l")
        normed_grad = add(term[0, 0], up_0, down_0, other_l)

    with jax.named_scope("input_out"):
        rows = checkpoint.astype(F32)
        inv_rms = lax.rsqrt(jnp.mean(rows * rows, axis=1, keepdims=True) + 1e-05)
        unit_rows = rows * inv_rms
        scaled = normed_grad * gain_f
        input_grad = (
            inv_rms * (scaled - unit_rows * jnp.mean(scaled * unit_rows, axis=1, keepdims=True))
        ).astype(BF)

    with jax.named_scope("weight_rows"):
        mine = qkv_weight.reshape(H, Z, C, T, fine, columns)
        mine = lax.dynamic_slice(mine, (0, z, c, 0, 0, 0), (H, 1, 1, T, fine, columns))
        mine = after(mine.reshape(H, T, fine, columns), part)
        mine = lax.all_to_all(mine.swapaxes(0, 1), TENSOR, 0, 0, tiled=True)

    with jax.named_scope("weight_out"):
        sums = after(sums, input_grad).reshape(H, T, fine, columns)
        dots = jnp.sum(sums.astype(F32) * mine.swapaxes(0, 1).astype(F32), axis=(1, 3))
        high = dots.astype(BF)
        low = (dots - high.astype(F32)).astype(BF)
        lane = lax.broadcasted_iota(jnp.int32, (H, T, fine, 128), 3)
        wide = lambda value: value[:, None, :, None]
        extra = jnp.where(lane == 0, wide(high), jnp.where(lane == 1, wide(low), 0))
        blocks = jnp.concatenate([sums, extra.astype(BF)], axis=3)
        blocks = lax.all_to_all(
            blocks.reshape(H * T, fine, columns + 128), ("h",) + TENSOR, 0, 0, tiled=True
        )
        blocks = blocks.reshape(H, T * fine, columns + 128).astype(F32)
        weight_out = jnp.sum(blocks[..., :columns], axis=0)
        dots = jnp.sum(blocks[..., columns:], axis=(0, 2))
        at = ((h * Z + z) * C + c) * (T * fine)
        gain_out = dots / lax.dynamic_slice_in_dim(gain_f, at, T * fine, 0)
    return (input_grad, gain_out, weight_out)


def solution(mesh):
    fine_mesh = Mesh(mesh.devices.reshape(H, Z, C, X, L), DP + TENSOR)
    rows = P(DP + TENSOR, None)
    in_specs = (rows, P(), P(None, TENSOR), P(DP, TENSOR))
    out_specs = (rows, P(DP), P(DP, TENSOR))
    return jax.shard_map(
        shards, mesh=fine_mesh, in_specs=in_specs, out_specs=out_specs, check_vma=False
    )
```

```python
import functools
import math

import jax
import jax.numpy as jnp
from jax import lax
from jax.experimental import pallas as pl
from jax.experimental.pallas import tpu as pltpu
from jax.sharding import Mesh
from jax.sharding import PartitionSpec as P

H, Z, C, X, L = 2, 8, 2, 4, 2
T = X * L
DP = ("h", "z", "c")
TENSOR = ("x", "l")
BF = jnp.bfloat16
F32 = jnp.float32

VMEM = pl.BlockSpec(memory_space=pltpu.VMEM)
SMEM = pl.BlockSpec(memory_space=pltpu.SMEM)
ANY = pl.BlockSpec(memory_space=pl.ANY)


def params(mib):
    return pltpu.CompilerParams(vmem_limit_bytes=mib << 20)


def cost(flops, bytes_accessed):
    return pl.CostEstimate(flops=flops, bytes_accessed=bytes_accessed, transcendentals=0)


def shift(value, axis, step):
    n = lax.axis_size(axis)
    return lax.ppermute(value, axis, [(i, (i + step) % n) for i in range(n)])


def swap(value, axis):
    return shift(value, axis, 1)


def relative(blocks, x, l):
    turned = lax.dynamic_slice_in_dim(jnp.concatenate([blocks, blocks], 0), x, X, 0)
    return jnp.where(l == 0, turned, turned[:, ::-1])


def after(values, *others):
    return lax.optimization_barrier((values, *others))[0]


def add(*values):
    total = values[0].astype(F32)
    for value in values[1:]:
        total = total + value.astype(F32)
    return total


def normed_kernel(z_ref, check_ref, gain_ref, out_ref, normed_ref):
    local, width = check_ref.shape
    span = width // (H * Z * C)
    fine = span // T
    per = 128 // fine
    values = check_ref[...].astype(F32)
    inv_rms = lax.rsqrt(jnp.mean(values * values, axis=1, keepdims=True) + 1e-05)
    normed_ref[...] = (values * inv_rms * gain_ref[...].astype(F32)).astype(BF)
    groups = Z * H // per
    lines = []
    for c in range(C):
        for group in range(groups):
            pieces = []
            for piece in range(per):
                k, h = divmod(group * per + piece, H)
                at = ((h * Z + lax.rem(z_ref[0] + k, Z)) * C + c) * span
                pieces.append(normed_ref[:, pl.ds(pl.multiple_of(at, span), span)])
            lines.append(jnp.concatenate(pieces, axis=1))
    stacked = jnp.concatenate(lines, axis=0)
    size = per * span
    row = lax.broadcasted_iota(jnp.int32, (size, size), 0)
    column = lax.broadcasted_iota(jnp.int32, (size, size), 1)
    k, t, i = row // span, (row // fine) % T, row % fine
    places = jnp.where(column == t * 128 + k * fine + i, 1.0, 0.0).astype(BF)
    placed = jnp.dot(stacked, places, preferred_element_type=F32).astype(BF)
    for c in range(C):
        for group in range(groups):
            at = (c * groups + group) * local
            for t in range(T):
                out_ref[c * T + t, :, group * 128 : (group + 1) * 128] = placed[
                    at : at + local, t * 128 : (t + 1) * 128
                ]


def normed_parts(z, checkpoint, gain):
    local, width = checkpoint.shape
    return pl.pallas_call(
        normed_kernel,
        in_specs=[SMEM, VMEM, VMEM],
        out_specs=VMEM,
        out_shape=jax.ShapeDtypeStruct((C * T, local, width // (C * T)), BF),
        scratch_shapes=[pltpu.VMEM((local, width), BF)],
        compiler_params=params(40),
        cost_estimate=cost(2 * local * width * 1024, 4 * local * width),
    )(z.reshape(1), checkpoint, gain.reshape(1, width))


def terms_kernel(count, cot_ref, w_ref, *refs):
    outs = refs[-count:]
    product = lax.dot_general(
        cot_ref[...], w_ref[...], (((1,), (1,)), ((), ())), preferred_element_type=F32
    ).astype(BF)
    rows = product.shape[0] // count
    for i, out in enumerate(outs):
        out[...] = product[i * rows : (i + 1) * rows]


def grad_terms(cot, weight, *tokens, tile=512):
    rows, depth = cot.shape
    width = weight.shape[0]
    own = rows // T
    return pl.pallas_call(
        functools.partial(terms_kernel, T),
        grid=(width // tile,),
        in_specs=[
            pl.BlockSpec((rows, depth), lambda i: (0, 0)),
            pl.BlockSpec((tile, depth), lambda i: (i, 0)),
        ]
        + [ANY] * len(tokens),
        out_specs=[pl.BlockSpec((own, tile), lambda i: (0, i))] * T,
        out_shape=[jax.ShapeDtypeStruct((own, width), BF)] * T,
        compiler_params=params(48),
        cost_estimate=cost(
            2 * rows * depth * width, 2 * (rows * depth + width * depth + rows * width)
        ),
    )(cot, weight, *tokens)


def weight_kernel(scale, count, core_ref, left_ref, *refs):
    outs = refs[-Z - 1 : -1]
    turned = refs[-1]
    tokens = left_ref.shape[1]

    @pl.when(pl.program_id(0) == 0)
    def _():
        turned[:, :tokens] = left_ref[core_ref[0]].T
        turned[:, tokens:] = left_ref[1 - core_ref[0]].T

    for i in range(count):

        @pl.when(pl.program_id(0) == i)
        def _():
            right = jnp.concatenate([refs[i][...], refs[count + i][...]], axis=0)
            product = jnp.dot(turned[...], right, preferred_element_type=F32)
            product = (product * scale).astype(BF)
            rows = product.shape[0] // Z
            for k, out in enumerate(outs):
                out[...] = product[k * rows : (k + 1) * rows].reshape(out.shape)


def weight_terms(core, left, own, other, scale, *tokens):
    cores, rows, features = left.shape
    columns = own[0].shape[1]
    count = len(own)
    fine = features // (Z * H)
    whole = lambda shape: pl.BlockSpec(shape, lambda i: (0,) * len(shape))
    return pl.pallas_call(
        functools.partial(weight_kernel, scale, count),
        grid=(count,),
        in_specs=[SMEM, whole(left.shape)]
        + [whole(own[0].shape)] * (2 * count)
        + [ANY] * len(tokens),
        out_specs=[pl.BlockSpec((H, 1, fine, columns), lambda i: (0, i, 0, 0))] * Z,
        out_shape=[jax.ShapeDtypeStruct((H, count, fine, columns), BF)] * Z,
        scratch_shapes=[pltpu.VMEM((features, cores * rows), BF)],
        compiler_params=params(48),
        cost_estimate=cost(
            2 * features * cores * rows * columns * count,
            2 * (features * cores * rows + (cores * rows + features) * columns * count),
        ),
    )(core.reshape(1), left, *own, *other, *tokens)


def sums_kernel(sizes, *refs):
    outs = refs[-len(sizes) :]
    at = 0
    for size, out in zip(sizes, outs):
        out[...] = add(*[ref[...] for ref in refs[at : at + size]]).astype(BF)
        at += size


def sums(groups, *tokens):
    values = [value for group in groups for value in group]
    return pl.pallas_call(
        functools.partial(sums_kernel, [len(group) for group in groups]),
        in_specs=[VMEM] * len(values) + [ANY] * len(tokens),
        out_specs=[VMEM] * len(groups),
        out_shape=[jax.ShapeDtypeStruct(group[0].shape, BF) for group in groups],
        compiler_params=params(32),
        cost_estimate=cost(values[0].size * len(values), 2 * values[0].size * len(values)),
    )(*values, *tokens)


def input_kernel(check_ref, gain_ref, a_ref, b_ref, c_ref, d_ref, *refs):
    out_ref = refs[-1]
    values = check_ref[...].astype(F32)
    inv_rms = lax.rsqrt(jnp.mean(values * values, axis=1, keepdims=True) + 1e-05)
    unit_rows = values * inv_rms
    scaled = add(a_ref[...], b_ref[...], c_ref[...], d_ref[...]) * gain_ref[...].astype(F32)
    mean = jnp.mean(scaled * unit_rows, axis=1, keepdims=True)
    out_ref[...] = (inv_rms * (scaled - unit_rows * mean)).astype(BF)


def input_out(checkpoint, gain, parts, *tokens):
    local, width = checkpoint.shape
    return pl.pallas_call(
        input_kernel,
        in_specs=[VMEM] * (2 + len(parts)) + [ANY] * len(tokens),
        out_specs=VMEM,
        out_shape=jax.ShapeDtypeStruct((local, width), BF),
        compiler_params=params(40),
        cost_estimate=cost(12 * local * width, 12 * local * width),
    )(checkpoint, gain.reshape(1, width), *parts, *tokens)


def blocks_kernel(order_ref, weight_ref, *refs):
    out_ref = refs[-1]
    columns = weight_ref.shape[-1]
    fine = weight_ref.shape[2]
    count = T // 2
    dots = [jnp.zeros((fine, 1), F32) for _ in range(H)]
    for i in range(T):
        terms = refs[3 * (i // count) : 3 * (i // count) + 3]
        t = order_ref[i]
        for h in range(H):
            value = add(*[term[h, i % count] for term in terms]).astype(BF)
            out_ref[h * T + t, :, :columns] = value
            product = value.astype(F32) * weight_ref[t, h].astype(F32)
            dots[h] += jnp.sum(product, axis=1, keepdims=True)
    lane = lax.broadcasted_iota(jnp.int32, (fine, 128), 1)
    for h in range(H):
        high = dots[h].astype(BF).astype(F32)
        extra = jnp.where(lane == 0, high, jnp.where(lane == 1, dots[h] - high, 0.0)).astype(BF)
        for t in range(T):
            out_ref[h * T + t, :, columns:] = extra


def last_blocks(order, weight, terms, *tokens):
    fine, columns = weight.shape[2:]
    return pl.pallas_call(
        blocks_kernel,
        in_specs=[SMEM] + [VMEM] * (1 + len(terms)) + [ANY] * len(tokens),
        out_specs=VMEM,
        out_shape=jax.ShapeDtypeStruct((H * T, fine, columns + 128), BF),
        compiler_params=params(32),
        cost_estimate=cost(5 * weight.size, 10 * weight.size),
    )(order, weight, *terms, *tokens)


def shards(checkpoint, gain, qkv_weight, qkv_cot):
    h, z, c = lax.axis_index("h"), lax.axis_index("z"), lax.axis_index("c")
    x, l = lax.axis_index("x"), lax.axis_index("l")
    local, width = checkpoint.shape
    tokens, columns = qkv_cot.shape
    grad_scale = 1.0 / math.sqrt(tokens * H * Z * C)
    fine = width // (H * Z * C * T)

    with jax.named_scope("normed_exchange"):
        parts = normed_parts(z, checkpoint, gain)
        left = lax.all_to_all(parts, ("c",) + TENSOR, 0, 0, tiled=True)
        left = left.reshape(C, tokens, Z * H * fine)

    with jax.named_scope("cot_gather"):
        near = {(0, 0): qkv_cot}
        near[0, 1] = swap(qkv_cot, "l")
        for step in (1, 3):
            near[step, 0] = shift(qkv_cot, "x", -step)
        near[2, 0] = shift(after(qkv_cot, parts), "x", -2)
        near[3, 1] = shift(near[0, 1], "x", 1)
        near[1, 1] = shift(near[0, 1], "x", -1)
        near[2, 1] = swap(near[2, 0], "l")
        across = {key: swap(value, "c") for key, value in near.items()}

    with jax.named_scope("input_terms"):
        cot_near = relative(qkv_cot.reshape(X, L, local, columns), x, l)
        term = grad_terms(cot_near.reshape(tokens, columns), qkv_weight, parts, near[0, 1])
        term = {(i // L, i % L): term[i] for i in range(T)}

    with jax.named_scope("weight_terms"):
        keys = (((0, 0), (0, 1), (1, 0), (3, 0)), ((2, 0), (1, 1), (3, 1), (2, 1)))
        product = lambda some, *given: weight_terms(
            c, left, [near[k] for k in some], [across[k] for k in some], grad_scale, *given
        )
        a = product(keys[0], term[0, 0])
        b = product(keys[1], a[0])

    with jax.named_scope("chains"):
        up = lambda value: shift(value, "z", 1)
        down = lambda value: shift(value, "z", -1)
        up_a, down_a = up(a[4]), down(a[5])
        far_up, far_down = shift(term[2, 0], "x", 1), shift(term[2, 1], "x", -1)
        up_1 = shift(term[1, 1], "x", 1)
        up_b, down_b = up(b[3]), down(b[4])
        s1 = sums([(a[3], up_a), (a[6], down_a)], b[0])
        up_a, down_a = up(s1[0]), down(s1[1])
        s2 = sums([(term[3, 1], far_down), (term[1, 0], far_up)], s1[0])
        down_1, up_0 = shift(s2[0], "x", -1), shift(s2[1], "x", 1)
        s3 = sums([(b[2], up_b), (b[5], down_b)], s2[0])
        up_b, down_b = up(s3[0]), down(s3[1])
        down_0 = shift(after(term[3, 0], s2[0]), "x", -1)
        s4 = sums([(a[2], up_a), (a[7], down_a)], s3[0])
        up_a, down_a = up(s4[0]), down(s4[1])
        s5 = sums([(b[1], up_b), (b[6], down_b)], s4[0])
        up_b, down_b = up(s5[0]), down(s5[1])
        s6 = sums([(a[1], up_a)], s5[0])
        up_a = up(s6[0])
        s7 = sums([(term[0, 1], up_1, down_1)], s6[0])
        other_l = swap(s7[0], "l")
        s8 = sums([(b[7], down_b)], s7[0])
        down_b = down(s8[0])

    with jax.named_scope("input_out"):
        input_grad = input_out(checkpoint, gain, (term[0, 0], up_0, down_0, other_l), s8[0])

    with jax.named_scope("weight_rows"):
        mine = qkv_weight.reshape(H, Z, C, T, fine, columns)
        mine = lax.dynamic_slice(mine, (0, z, c, 0, 0, 0), (H, 1, 1, T, fine, columns))
        mine = after(mine.reshape(H, T, fine, columns), b[0])
        mine = lax.all_to_all(mine.swapaxes(0, 1), TENSOR, 0, 0, tiled=True)

    with jax.named_scope("weight_out"):
        order = jnp.stack(
            [lax.rem(x + i, X) * L + lax.rem(l + j, L) for some in keys for i, j in some]
        )
        blocks = last_blocks(order, mine, (a[0], up_a, down_a, b[0], up_b, down_b), s8[0])
        blocks = lax.all_to_all(blocks, ("h",) + TENSOR, 0, 0, tiled=True)
        blocks = blocks.reshape(H, T * fine, columns + 128).astype(F32)
        weight_out = jnp.sum(blocks[..., :columns], axis=0)
        dots = jnp.sum(blocks[..., columns:], axis=(0, 2))
        at = ((h * Z + z) * C + c) * (T * fine)
        gain_out = dots / lax.dynamic_slice_in_dim(gain, at, T * fine, 0).astype(F32)
    return (input_grad, gain_out, weight_out)


def solution(mesh):
    fine_mesh = Mesh(mesh.devices.reshape(H, Z, C, X, L), DP + TENSOR)
    rows = P(DP + TENSOR, None)
    in_specs = (rows, P(), P(None, TENSOR), P(DP, TENSOR))
    out_specs = (rows, P(DP), P(DP, TENSOR))
    return jax.shard_map(
        shards, mesh=fine_mesh, in_specs=in_specs, out_specs=out_specs, check_vma=False
    )
```

```python
import functools
import math

import jax
import jax.numpy as jnp
from jax import lax
from jax.experimental import pallas as pl
from jax.experimental.pallas import tpu as pltpu
from jax.sharding import Mesh
from jax.sharding import PartitionSpec as P

H, Z, C, X, L = 2, 8, 2, 4, 2
T = X * L
DP = ("h", "z", "c")
TENSOR = ("x", "l")
BF = jnp.bfloat16
F32 = jnp.float32

VMEM = pl.BlockSpec(memory_space=pltpu.VMEM)
SMEM = pl.BlockSpec(memory_space=pltpu.SMEM)
ANY = pl.BlockSpec(memory_space=pl.ANY)


def params(mib):
    return pltpu.CompilerParams(vmem_limit_bytes=mib << 20)


COST = pl.CostEstimate(flops=1000, bytes_accessed=1000, transcendentals=0)


def shift(value, axis, step):
    n = lax.axis_size(axis)
    return lax.ppermute(value, axis, [(i, (i + step) % n) for i in range(n)])


def swap(value, axis):
    return shift(value, axis, 1)


def after(values, *others):
    return lax.optimization_barrier((values, *others))[0]


def add(*values):
    total = values[0].astype(F32)
    for value in values[1:]:
        total = total + value.astype(F32)
    return total


def normed_kernel(z_ref, check_ref, gain_ref, out_ref, normed_ref):
    local, width = check_ref.shape
    span = width // (H * Z * C)
    fine = span // T
    per = 128 // fine
    values = check_ref[...].astype(F32)
    inv_rms = lax.rsqrt(jnp.mean(values * values, axis=1, keepdims=True) + 1e-05)
    normed_ref[...] = (values * inv_rms * gain_ref[...].astype(F32)).astype(BF)
    groups = Z * H // per
    lines = []
    for c in range(C):
        for group in range(groups):
            pieces = []
            for piece in range(per):
                k, h = divmod(group * per + piece, H)
                at = ((h * Z + lax.rem(z_ref[0] + k, Z)) * C + c) * span
                pieces.append(normed_ref[:, pl.ds(pl.multiple_of(at, span), span)])
            lines.append(jnp.concatenate(pieces, axis=1))
    stacked = jnp.concatenate(lines, axis=0)
    size = per * span
    row = lax.broadcasted_iota(jnp.int32, (size, size), 0)
    column = lax.broadcasted_iota(jnp.int32, (size, size), 1)
    k, t, i = row // span, (row // fine) % T, row % fine
    places = jnp.where(column == t * 128 + k * fine + i, 1.0, 0.0).astype(BF)
    placed = jnp.dot(stacked, places, preferred_element_type=F32).astype(BF)
    for c in range(C):
        for group in range(groups):
            at = (c * groups + group) * local
            for t in range(T):
                out_ref[c * T + t, :, group * 128 : (group + 1) * 128] = placed[
                    at : at + local, t * 128 : (t + 1) * 128
                ]


def normed_parts(z, checkpoint, gain):
    local, width = checkpoint.shape
    return pl.pallas_call(
        normed_kernel,
        in_specs=[SMEM, VMEM, VMEM],
        out_specs=VMEM,
        out_shape=jax.ShapeDtypeStruct((C * T, local, width // (C * T)), BF),
        scratch_shapes=[pltpu.VMEM((local, width), BF)],
        compiler_params=params(20),
        cost_estimate=COST,
    )(z.reshape(1), checkpoint, gain)


def terms_kernel(cot_ref, w_ref, *refs):
    out, token = refs[-2:]
    token[...] = jnp.zeros(token.shape, F32)
    product = lax.dot_general(
        cot_ref[...], w_ref[...], (((1,), (1,)), ((), ())), preferred_element_type=F32
    )
    out[...] = product.astype(BF)


def grad_terms(cot, weight, *tokens, tile=2048):
    rows, depth = cot.shape
    width = weight.shape[0]
    return pl.pallas_call(
        terms_kernel,
        grid=(width // tile,),
        in_specs=[
            pl.BlockSpec((rows, depth), lambda i: (0, 0)),
            pl.BlockSpec((tile, depth), lambda i: (i, 0)),
        ]
        + [ANY] * len(tokens),
        out_specs=[
            pl.BlockSpec((rows, tile), lambda i: (0, i)),
            pl.BlockSpec((8, 128), lambda i: (0, 0)),
        ],
        out_shape=[
            jax.ShapeDtypeStruct((rows, width), BF),
            jax.ShapeDtypeStruct((8, 128), F32),
        ],
        compiler_params=params(55),
        cost_estimate=COST,
    )(cot, weight, *tokens)


def weight_kernel(scale, count, core_ref, left_ref, *refs):
    outs = refs[-Z - 1 : -1]
    turned = refs[-1]
    tokens = left_ref.shape[1]

    @pl.when(pl.program_id(0) == 0)
    def _():
        turned[:, :tokens] = left_ref[core_ref[0]].T
        turned[:, tokens:] = left_ref[1 - core_ref[0]].T

    for i in range(count):

        @pl.when(pl.program_id(0) == i)
        def _():
            right = jnp.concatenate([refs[i][...], refs[count + i][...]], axis=0)
            product = jnp.dot(turned[...], right, preferred_element_type=F32)
            product = (product * scale).astype(BF)
            rows = product.shape[0] // Z
            for k, out in enumerate(outs):
                out[...] = product[k * rows : (k + 1) * rows].reshape(out.shape)


def weight_terms(core, left, own, other, scale, *tokens):
    cores, rows, features = left.shape
    columns = own[0].shape[1]
    count = len(own)
    fine = features // (Z * H)
    whole = lambda shape: pl.BlockSpec(shape, lambda i: (0,) * len(shape))
    return pl.pallas_call(
        functools.partial(weight_kernel, scale, count),
        grid=(count,),
        in_specs=[SMEM, whole(left.shape)]
        + [whole(own[0].shape)] * (2 * count)
        + [ANY] * len(tokens),
        out_specs=[pl.BlockSpec((H, 1, fine, columns), lambda i: (0, i, 0, 0))] * Z,
        out_shape=[jax.ShapeDtypeStruct((H, count, fine, columns), BF)] * Z,
        scratch_shapes=[pltpu.VMEM((features, cores * rows), BF)],
        compiler_params=params(24),
        cost_estimate=COST,
    )(core.reshape(1), left, *own, *other, *tokens)


def sums_kernel(sizes, *refs):
    outs = refs[-len(sizes) :]
    at = 0
    for size, out in zip(sizes, outs):
        out[...] = add(*[ref[...] for ref in refs[at : at + size]]).astype(BF)
        at += size


def sums(groups, *tokens):
    values = [value for group in groups for value in group]
    return pl.pallas_call(
        functools.partial(sums_kernel, [len(group) for group in groups]),
        in_specs=[VMEM] * len(values) + [ANY] * len(tokens),
        out_specs=[VMEM] * len(groups),
        out_shape=[jax.ShapeDtypeStruct(group[0].shape, BF) for group in groups],
        compiler_params=params(8),
        cost_estimate=COST,
    )(*values, *tokens)


def input_kernel(check_ref, gain_ref, terms_ref, out_ref):
    values = check_ref[...].astype(F32)
    inv_rms = lax.rsqrt(jnp.mean(values * values, axis=1, keepdims=True) + 1e-05)
    unit_rows = values * inv_rms
    scaled = add(*[terms_ref[t] for t in range(T)]) * gain_ref[...].astype(F32)
    mean = jnp.mean(scaled * unit_rows, axis=1, keepdims=True)
    out_ref[...] = (inv_rms * (scaled - unit_rows * mean)).astype(BF)


def input_out(checkpoint, gain, terms, rows=16):
    local, width = checkpoint.shape
    return pl.pallas_call(
        input_kernel,
        grid=(local // rows,),
        in_specs=[
            pl.BlockSpec((rows, width), lambda i: (i, 0)),
            pl.BlockSpec((1, width), lambda i: (0, 0)),
            pl.BlockSpec((T, rows, width), lambda i: (0, i, 0)),
        ],
        out_specs=pl.BlockSpec((rows, width), lambda i: (i, 0)),
        out_shape=jax.ShapeDtypeStruct((local, width), BF),
        compiler_params=params(24),
        cost_estimate=COST,
    )(checkpoint, gain, terms)


def blocks_kernel(order_ref, weight_ref, *refs):
    out_ref = refs[-1]
    columns = weight_ref.shape[-1]
    fine = weight_ref.shape[2]
    count = T // 2
    dots = [jnp.zeros((fine, 1), F32) for _ in range(H)]
    for i in range(T):
        terms = refs[3 * (i // count) : 3 * (i // count) + 3]
        t = order_ref[i]
        for h in range(H):
            value = add(*[term[h, i % count] for term in terms]).astype(BF)
            out_ref[h * T + t, :, :columns] = value
            product = value.astype(F32) * weight_ref[t, h].astype(F32)
            dots[h] += jnp.sum(product, axis=1, keepdims=True)
    lane = lax.broadcasted_iota(jnp.int32, (fine, 128), 1)
    for h in range(H):
        high = dots[h].astype(BF).astype(F32)
        extra = jnp.where(lane == 0, high, jnp.where(lane == 1, dots[h] - high, 0.0)).astype(BF)
        for t in range(T):
            out_ref[h * T + t, :, columns:] = extra


def last_blocks(order, weight, terms, *tokens):
    fine, columns = weight.shape[2:]
    return pl.pallas_call(
        blocks_kernel,
        in_specs=[SMEM] + [VMEM] * (1 + len(terms)) + [ANY] * len(tokens),
        out_specs=VMEM,
        out_shape=jax.ShapeDtypeStruct((H * T, fine, columns + 128), BF),
        compiler_params=params(8),
        cost_estimate=COST,
    )(order, weight, *terms, *tokens)


def finish_kernel(group_ref, gain_ref, blocks_ref, weight_ref, gain_out_ref):
    columns = weight_ref.shape[1]
    fine = blocks_ref.shape[1]
    lane = lax.broadcasted_iota(jnp.int32, (8, 128), 1)
    pick = jnp.where(lane < 2, 1.0, 0.0).astype(BF)
    dots = jnp.zeros((8, weight_ref.shape[0]), F32)
    for h in range(H):
        extra = blocks_ref[h * T : (h + 1) * T, :, columns:].reshape(T * fine, 128)
        dots += lax.dot_general(pick, extra, (((1,), (1,)), ((), ())), preferred_element_type=F32)
    gain_out_ref[...] = dots[:1] / gain_ref[pl.ds(group_ref[0], 1), :].astype(F32)
    for t in range(T):
        weight_ref[t * fine : (t + 1) * fine] = add(
            *[blocks_ref[h * T + t, :, :columns] for h in range(H)]
        )


def finish(group, gain, blocks):
    fine, width = blocks.shape[1:]
    rows = T * fine
    weight, gain_row = pl.pallas_call(
        finish_kernel,
        in_specs=[SMEM, VMEM, VMEM],
        out_specs=[VMEM, VMEM],
        out_shape=[
            jax.ShapeDtypeStruct((rows, width - 128), F32),
            jax.ShapeDtypeStruct((1, rows), F32),
        ],
        compiler_params=params(8),
        cost_estimate=COST,
    )(group.reshape(1), gain.astype(F32).reshape(-1, rows), blocks)
    return weight, gain_row.reshape(rows)


def shards(checkpoint, gain, qkv_weight, qkv_cot):
    h, z, c = lax.axis_index("h"), lax.axis_index("z"), lax.axis_index("c")
    x, l = lax.axis_index("x"), lax.axis_index("l")
    local, width = checkpoint.shape
    tokens, columns = qkv_cot.shape
    grad_scale = 1.0 / math.sqrt(tokens * H * Z * C)
    fine = width // (H * Z * C * T)
    gain_row = gain.reshape(1, width)

    with jax.named_scope("normed_exchange"):
        parts = normed_parts(z, checkpoint, gain_row)
        left = lax.all_to_all(parts, ("c",) + TENSOR, 0, 0, tiled=True)
        left = left.reshape(C, tokens, Z * H * fine)

    with jax.named_scope("cot_gather"):
        near = {(0, 0): qkv_cot}
        near[0, 1] = swap(qkv_cot, "l")
        for step in (1, 3):
            near[step, 0] = shift(qkv_cot, "x", -step)
        near[2, 0] = shift(after(qkv_cot, parts), "x", -2)
        near[3, 1] = shift(near[0, 1], "x", 1)
        near[1, 1] = shift(near[0, 1], "x", -1)
        near[2, 1] = swap(near[2, 0], "l")
        across = {key: swap(value, "c") for key, value in near.items()}

    with jax.named_scope("input_terms"):
        term, multiplied = grad_terms(qkv_cot, qkv_weight, parts)

    with jax.named_scope("weight_terms"):
        keys = (((0, 0), (0, 1), (1, 0), (3, 0)), ((2, 0), (1, 1), (3, 1), (2, 1)))
        product = lambda some, *given: weight_terms(
            c, left, [near[k] for k in some], [across[k] for k in some], grad_scale, *given
        )
        a = product(keys[0], multiplied)
        b = product(keys[1], a[0])

    with jax.named_scope("weight_rows"):
        mine = qkv_weight.reshape(H, Z, C, T, fine, columns)
        mine = lax.dynamic_slice(mine, (0, z, c, 0, 0, 0), (H, 1, 1, T, fine, columns))
        mine = after(mine.reshape(H, T, fine, columns), left)
        mine = lax.all_to_all(mine.swapaxes(0, 1), TENSOR, 0, 0, tiled=True)

    with jax.named_scope("input_exchange"):
        term = after(term, near[1, 1], near[3, 1], near[2, 1], mine, a[0])
        term = lax.all_to_all(term, TENSOR, 0, 0, tiled=True)
        input_grad = input_out(checkpoint, gain_row, term.reshape(T, local, width))

    with jax.named_scope("chains"):
        up = lambda value: shift(value, "z", 1)
        down = lambda value: shift(value, "z", -1)
        up_a, down_a = up(a[4]), down(a[5])
        up_b, down_b = up(b[3]), down(b[4])
        s1 = sums([(a[3], up_a), (a[6], down_a)], b[0])
        up_a, down_a = up(s1[0]), down(s1[1])
        s2 = sums([(b[2], up_b), (b[5], down_b)], s1[0])
        up_b, down_b = up(s2[0]), down(s2[1])
        s3 = sums([(a[2], up_a), (a[7], down_a)], s2[0])
        up_a, down_a = up(s3[0]), down(s3[1])
        s4 = sums([(b[1], up_b), (b[6], down_b)], s3[0])
        up_b, down_b = up(s4[0]), down(s4[1])
        s5 = sums([(a[1], up_a)], s4[0])
        up_a = up(s5[0])
        s6 = sums([(b[7], down_b)], s5[0])
        down_b = down(s6[0])

    with jax.named_scope("weight_out"):
        order = jnp.stack(
            [lax.rem(x + i, X) * L + lax.rem(l + j, L) for some in keys for i, j in some]
        )
        blocks = last_blocks(order, mine, (a[0], up_a, down_a, b[0], up_b, down_b), term[:8, :128])
        blocks = lax.all_to_all(blocks, ("h",) + TENSOR, 0, 0, tiled=True)
        weight_out, gain_out = finish((h * Z + z) * C + c, gain, blocks)
    return (input_grad, gain_out, weight_out)


def solution(mesh):
    fine_mesh = Mesh(mesh.devices.reshape(H, Z, C, X, L), DP + TENSOR)
    rows = P(DP + TENSOR, None)
    in_specs = (rows, P(), P(None, TENSOR), P(DP, TENSOR))
    out_specs = (rows, P(DP), P(DP, TENSOR))
    return jax.shard_map(
        shards, mesh=fine_mesh, in_specs=in_specs, out_specs=out_specs, check_vma=False
    )
```

```python
import functools
import math

import jax
import jax.numpy as jnp
from jax import lax
from jax.experimental import pallas as pl
from jax.experimental.pallas import tpu as pltpu
from jax.sharding import Mesh
from jax.sharding import PartitionSpec as P

H, Z, C, X, L = 2, 8, 2, 4, 2
T = X * L
DP = ("h", "z", "c")
TENSOR = ("x", "l")
BF = jnp.bfloat16
F32 = jnp.float32

VMEM = pl.BlockSpec(memory_space=pltpu.VMEM)
SMEM = pl.BlockSpec(memory_space=pltpu.SMEM)
ANY = pl.BlockSpec(memory_space=pl.ANY)


def params(mib):
    return pltpu.CompilerParams(vmem_limit_bytes=mib << 20)


def cost(flops, bytes_accessed):
    return pl.CostEstimate(flops=flops, bytes_accessed=bytes_accessed, transcendentals=0)


def shift(value, axis, step):
    n = lax.axis_size(axis)
    return lax.ppermute(value, axis, [(i, (i + step) % n) for i in range(n)])


def swap(value, axis):
    return shift(value, axis, 1)


def relative(blocks, x, l):
    turned = lax.dynamic_slice_in_dim(jnp.concatenate([blocks, blocks], 0), x, X, 0)
    return jnp.where(l == 0, turned, turned[:, ::-1])


def after(values, *others):
    return lax.optimization_barrier((values, *others))[0]


def add(*values):
    total = values[0].astype(F32)
    for value in values[1:]:
        total = total + value.astype(F32)
    return total


def normed_kernel(z_ref, check_ref, gain_ref, out_ref, normed_ref):
    local, width = check_ref.shape
    span = width // (H * Z * C)
    fine = span // T
    per = 128 // fine
    values = check_ref[...].astype(F32)
    inv_rms = lax.rsqrt(jnp.mean(values * values, axis=1, keepdims=True) + 1e-05)
    normed_ref[...] = (values * inv_rms * gain_ref[...].astype(F32)).astype(BF)
    groups = Z * H // per
    lines = []
    for c in range(C):
        for group in range(groups):
            pieces = []
            for piece in range(per):
                k, h = divmod(group * per + piece, H)
                at = ((h * Z + lax.rem(z_ref[0] + k, Z)) * C + c) * span
                pieces.append(normed_ref[:, pl.ds(pl.multiple_of(at, span), span)])
            lines.append(jnp.concatenate(pieces, axis=1))
    stacked = jnp.concatenate(lines, axis=0)
    size = per * span
    row = lax.broadcasted_iota(jnp.int32, (size, size), 0)
    column = lax.broadcasted_iota(jnp.int32, (size, size), 1)
    k, t, i = row // span, (row // fine) % T, row % fine
    places = jnp.where(column == t * 128 + k * fine + i, 1.0, 0.0).astype(BF)
    placed = jnp.dot(stacked, places, preferred_element_type=F32).astype(BF)
    for c in range(C):
        for group in range(groups):
            at = (c * groups + group) * local
            for t in range(T):
                out_ref[c * T + t, :, group * 128 : (group + 1) * 128] = placed[
                    at : at + local, t * 128 : (t + 1) * 128
                ]


def normed_parts(z, checkpoint, gain):
    local, width = checkpoint.shape
    return pl.pallas_call(
        normed_kernel,
        in_specs=[SMEM, VMEM, VMEM],
        out_specs=VMEM,
        out_shape=jax.ShapeDtypeStruct((C * T, local, width // (C * T)), BF),
        scratch_shapes=[pltpu.VMEM((local, width), BF)],
        compiler_params=params(20),
        cost_estimate=cost(2 * local * width * 1024, 4 * local * width),
    )(z.reshape(1), checkpoint, gain)


def terms_kernel(cot_ref, w_ref, *refs):
    outs, token = refs[-T - 1 : -1], refs[-1]
    token[...] = jnp.zeros(token.shape, F32)
    product = lax.dot_general(
        cot_ref[...], w_ref[...], (((1,), (1,)), ((), ())), preferred_element_type=F32
    )
    rows = product.shape[0] // T
    for i, out in enumerate(outs):
        out[...] = product[i * rows : (i + 1) * rows].astype(BF)


def grad_terms(cot, weight, *tokens, tile=2048):
    rows, depth = cot.shape
    width = weight.shape[0]
    own = rows // T
    outs = pl.pallas_call(
        terms_kernel,
        grid=(width // tile,),
        in_specs=[
            pl.BlockSpec((rows, depth), lambda i: (0, 0)),
            pl.BlockSpec((tile, depth), lambda i: (i, 0)),
        ]
        + [ANY] * len(tokens),
        out_specs=[pl.BlockSpec((own, tile), lambda i: (0, i))] * T
        + [pl.BlockSpec((8, 128), lambda i: (0, 0))],
        out_shape=[jax.ShapeDtypeStruct((own, width), BF)] * T
        + [jax.ShapeDtypeStruct((8, 128), F32)],
        compiler_params=params(58),
        cost_estimate=cost(
            4 * rows * depth * width, 2 * (rows * depth + width * depth + rows * width)
        ),
    )(cot, weight, *tokens)
    return outs[:T], outs[T]


def weight_kernel(scale, count, core_ref, left_ref, *refs):
    outs = refs[-Z - 1 : -1]
    turned = refs[-1]
    tokens = left_ref.shape[1]

    @pl.when(pl.program_id(0) == 0)
    def _():
        turned[:, :tokens] = left_ref[core_ref[0]].T
        turned[:, tokens:] = left_ref[1 - core_ref[0]].T

    for i in range(count):

        @pl.when(pl.program_id(0) == i)
        def _():
            right = jnp.concatenate([refs[i][...], refs[count + i][...]], axis=0)
            product = jnp.dot(turned[...], right, preferred_element_type=F32)
            product = (product * scale).astype(BF)
            rows = product.shape[0] // Z
            for k, out in enumerate(outs):
                out[...] = product[k * rows : (k + 1) * rows].reshape(out.shape)


def weight_terms(core, left, own, other, scale, *tokens):
    cores, rows, features = left.shape
    columns = own[0].shape[1]
    count = len(own)
    fine = features // (Z * H)
    whole = lambda shape: pl.BlockSpec(shape, lambda i: (0,) * len(shape))
    return pl.pallas_call(
        functools.partial(weight_kernel, scale, count),
        grid=(count,),
        in_specs=[SMEM, whole(left.shape)]
        + [whole(own[0].shape)] * (2 * count)
        + [ANY] * len(tokens),
        out_specs=[pl.BlockSpec((H, 1, fine, columns), lambda i: (0, i, 0, 0))] * Z,
        out_shape=[jax.ShapeDtypeStruct((H, count, fine, columns), BF)] * Z,
        scratch_shapes=[pltpu.VMEM((features, cores * rows), BF)],
        compiler_params=params(58),
        cost_estimate=cost(
            2 * features * cores * rows * columns * count,
            2 * (features * cores * rows + (cores * rows + features) * columns * count),
        ),
    )(core.reshape(1), left, *own, *other, *tokens)


def sums_kernel(sizes, *refs):
    outs = refs[-len(sizes) :]
    at = 0
    for size, out in zip(sizes, outs):
        out[...] = add(*[ref[...] for ref in refs[at : at + size]]).astype(BF)
        at += size


def sums(groups, *tokens, steps=1):
    values = [value for group in groups for value in group]
    shape = values[0].shape
    block = shape[:-1] + (shape[-1] // steps,)
    spec = pl.BlockSpec(block, lambda i: (0,) * (len(shape) - 1) + (i,))
    return pl.pallas_call(
        functools.partial(sums_kernel, [len(group) for group in groups]),
        grid=(steps,),
        in_specs=[spec] * len(values) + [ANY] * len(tokens),
        out_specs=[spec] * len(groups),
        out_shape=[jax.ShapeDtypeStruct(shape, BF) for group in groups],
        compiler_params=params(16),
        cost_estimate=cost(values[0].size * len(values), 2 * values[0].size * len(values)),
    )(*values, *tokens)


def input_kernel(check_ref, gain_ref, *refs):
    out_ref = refs[-1]
    values = check_ref[...].astype(F32)
    inv_rms = lax.rsqrt(jnp.mean(values * values, axis=1, keepdims=True) + 1e-05)
    unit_rows = values * inv_rms
    scaled = add(*[ref[...] for ref in refs[:4]]) * gain_ref[...].astype(F32)
    mean = jnp.mean(scaled * unit_rows, axis=1, keepdims=True)
    out_ref[...] = (inv_rms * (scaled - unit_rows * mean)).astype(BF)


def input_out(checkpoint, gain, parts, *tokens, rows=16):
    local, width = checkpoint.shape
    spec = pl.BlockSpec((rows, width), lambda i: (i, 0))
    return pl.pallas_call(
        input_kernel,
        grid=(local // rows,),
        in_specs=[spec, pl.BlockSpec((1, width), lambda i: (0, 0))]
        + [spec] * len(parts)
        + [ANY] * len(tokens),
        out_specs=spec,
        out_shape=jax.ShapeDtypeStruct((local, width), BF),
        compiler_params=params(24),
        cost_estimate=cost(12 * local * width, 12 * local * width),
    )(checkpoint, gain, *parts, *tokens)


def blocks_kernel(order_ref, weight_ref, *refs):
    out_ref = refs[-1]
    columns = weight_ref.shape[-1]
    fine = weight_ref.shape[2]
    count = T // 2
    dots = [jnp.zeros((fine, 1), F32) for _ in range(H)]
    for i in range(T):
        terms = refs[3 * (i // count) : 3 * (i // count) + 3]
        t = order_ref[i]
        for h in range(H):
            value = add(*[term[h, i % count] for term in terms]).astype(BF)
            out_ref[h * T + t, :, :columns] = value
            product = value.astype(F32) * weight_ref[t, h].astype(F32)
            dots[h] += jnp.sum(product, axis=1, keepdims=True)
    lane = lax.broadcasted_iota(jnp.int32, (fine, 128), 1)
    for h in range(H):
        high = dots[h].astype(BF).astype(F32)
        extra = jnp.where(lane == 0, high, jnp.where(lane == 1, dots[h] - high, 0.0)).astype(BF)
        for t in range(T):
            out_ref[h * T + t, :, columns:] = extra


def last_blocks(order, weight, terms, *tokens):
    fine, columns = weight.shape[2:]
    return pl.pallas_call(
        blocks_kernel,
        in_specs=[SMEM] + [VMEM] * (1 + len(terms)) + [ANY] * len(tokens),
        out_specs=VMEM,
        out_shape=jax.ShapeDtypeStruct((H * T, fine, columns + 128), BF),
        compiler_params=params(8),
        cost_estimate=cost(5 << 20, 5 << 20),
    )(order, weight, *terms, *tokens)


def finish_kernel(group_ref, gain_ref, blocks_ref, weight_ref, gain_out_ref):
    columns = weight_ref.shape[1]
    fine = blocks_ref.shape[1]
    lane = lax.broadcasted_iota(jnp.int32, (8, 128), 1)
    pick = jnp.where(lane < 2, 1.0, 0.0).astype(BF)
    dots = jnp.zeros((8, weight_ref.shape[0]), F32)
    for h in range(H):
        extra = blocks_ref[h * T : (h + 1) * T, :, columns:].reshape(T * fine, 128)
        dots += lax.dot_general(pick, extra, (((1,), (1,)), ((), ())), preferred_element_type=F32)
    gain_out_ref[...] = dots[:1] / gain_ref[pl.ds(group_ref[0], 1), :].astype(F32)
    for t in range(T):
        weight_ref[t * fine : (t + 1) * fine] = add(
            *[blocks_ref[h * T + t, :, :columns] for h in range(H)]
        )


def finish(group, gain, blocks):
    fine, width = blocks.shape[1:]
    rows = T * fine
    weight, gain_row = pl.pallas_call(
        finish_kernel,
        in_specs=[SMEM, VMEM, VMEM],
        out_specs=[VMEM, VMEM],
        out_shape=[
            jax.ShapeDtypeStruct((rows, width - 128), F32),
            jax.ShapeDtypeStruct((1, rows), F32),
        ],
        compiler_params=params(8),
        cost_estimate=cost(5 << 20, 5 << 20),
    )(group.reshape(1), gain.astype(F32).reshape(-1, rows), blocks)
    return weight, gain_row.reshape(rows)


def shards(checkpoint, gain, qkv_weight, qkv_cot):
    h, z, c = lax.axis_index("h"), lax.axis_index("z"), lax.axis_index("c")
    x, l = lax.axis_index("x"), lax.axis_index("l")
    local, width = checkpoint.shape
    tokens, columns = qkv_cot.shape
    grad_scale = 1.0 / math.sqrt(tokens * H * Z * C)
    fine = width // (H * Z * C * T)
    gain_row = gain.reshape(1, width)

    with jax.named_scope("normed_exchange"):
        parts = normed_parts(z, checkpoint, gain_row)
        left = lax.all_to_all(parts, ("c",) + TENSOR, 0, 0, tiled=True)
        left = left.reshape(C, tokens, Z * H * fine)

    near = {(0, 0): qkv_cot}
    with jax.named_scope("cot_gather"):
        near[0, 1] = swap(qkv_cot, "l")
        for step in (1, 3, 2):
            near[step, 0] = shift(qkv_cot, "x", -step)

    with jax.named_scope("input_terms"):
        cot_near = relative(qkv_cot.reshape(X, L, local, columns), x, l)
        term, multiplied = grad_terms(cot_near.reshape(tokens, columns), qkv_weight, parts)

    keys = (((0, 0), (0, 1), (1, 0), (3, 0)), ((2, 0), (1, 1), (3, 1), (2, 1)))
    across = {(0, 0): swap(qkv_cot, "c")}

    def product(some, *given):
        own, other = [near[key] for key in some], [across[key] for key in some]
        return weight_terms(c, left, own, other, grad_scale, *given)

    with jax.named_scope("cot_gather"):
        for key in ((0, 1), (1, 0), (3, 0), (2, 0)):
            near[key] = after(near[key], multiplied, left)
        near[3, 1] = shift(near[0, 1], "x", 1)
        near[1, 1] = shift(near[0, 1], "x", -1)
        near[2, 1] = swap(near[2, 0], "l")
        for key in keys[0][1:]:
            across[key] = swap(near[key], "c")
    with jax.named_scope("weight_terms"):
        a = product(keys[0], multiplied)
    with jax.named_scope("cot_gather"):
        for key in keys[1]:
            near[key] = after(near[key], a[0])
            across[key] = swap(near[key], "c")
    with jax.named_scope("weight_terms"):
        b = product(keys[1], a[0])

    with jax.named_scope("chains"):
        up = lambda value: shift(value, "z", 1)
        down = lambda value: shift(value, "z", -1)
        term = after(term, near[1, 1], near[3, 1])
        term = {(i // L, i % L): term[i] for i in range(T)}
        up_a, down_a = up(a[4]), down(a[5])
        far_up, far_down = shift(term[2, 0], "x", 1), shift(term[2, 1], "x", -1)
        up_1 = shift(term[1, 1], "x", 1)
        up_b, down_b = up(b[3]), down(b[4])
        s1 = sums([(a[3], up_a), (a[6], down_a)], b[0])
        up_a, down_a = up(s1[0]), down(s1[1])
        s2 = sums([(term[3, 1], far_down), (term[1, 0], far_up)], s1[0], steps=4)
        down_1, up_0 = shift(s2[0], "x", -1), shift(s2[1], "x", 1)
        down_0 = shift(after(term[3, 0], s2[0]), "x", -1)
        s3 = sums([(b[2], up_b), (b[5], down_b)], s2[0])
        up_b, down_b = up(s3[0]), down(s3[1])
        s4 = sums([(a[2], up_a), (a[7], down_a)], s3[0])
        up_a, down_a = up(s4[0]), down(s4[1])
        s5 = sums([(b[1], up_b), (b[6], down_b)], s4[0])
        up_b, down_b = up(s5[0]), down(s5[1])
        s6 = sums([(term[0, 1], up_1, down_1)], s5[0], steps=4)
        other_l = swap(s6[0], "l")
        s7 = sums([(a[1], up_a)], s6[0])
        up_a = up(s7[0])
        s8 = sums([(b[7], down_b)], s7[0])
        down_b = down(s8[0])

    with jax.named_scope("weight_rows"):
        mine = qkv_weight.reshape(H, Z, C, T, fine, columns)
        mine = lax.dynamic_slice(mine, (0, z, c, 0, 0, 0), (H, 1, 1, T, fine, columns))
        mine = after(mine.reshape(H, T, fine, columns), s3[0])
        mine = lax.all_to_all(mine.swapaxes(0, 1), TENSOR, 0, 0, tiled=True)

    with jax.named_scope("input_out"):
        input_grad = input_out(checkpoint, gain_row, (term[0, 0], up_0, down_0, other_l), s8[0])

    with jax.named_scope("weight_out"):
        order = jnp.stack(
            [lax.rem(x + i, X) * L + lax.rem(l + j, L) for some in keys for i, j in some]
        )
        blocks = last_blocks(order, mine, (a[0], up_a, down_a, b[0], up_b, down_b))
        blocks = lax.all_to_all(blocks, ("h",) + TENSOR, 0, 0, tiled=True)
        weight_out, gain_out = finish((h * Z + z) * C + c, gain, blocks)
    return (input_grad, gain_out, weight_out)


def solution(mesh):
    fine_mesh = Mesh(mesh.devices.reshape(H, Z, C, X, L), DP + TENSOR)
    rows = P(DP + TENSOR, None)
    in_specs = (rows, P(), P(None, TENSOR), P(DP, TENSOR))
    out_specs = (rows, P(DP), P(DP, TENSOR))
    return jax.shard_map(
        shards, mesh=fine_mesh, in_specs=in_specs, out_specs=out_specs, check_vma=False
    )
```

```python
import functools
import math

import jax
import jax.numpy as jnp
from jax import lax
from jax.experimental import pallas as pl
from jax.experimental.pallas import tpu as pltpu
from jax.sharding import Mesh
from jax.sharding import PartitionSpec as P

H, Z, C, X, L = 2, 8, 2, 4, 2
T = X * L
DP = ("h", "z", "c")
TENSOR = ("x", "l")
BF = jnp.bfloat16
F32 = jnp.float32

VMEM = pl.BlockSpec(memory_space=pltpu.VMEM)
SMEM = pl.BlockSpec(memory_space=pltpu.SMEM)
ANY = pl.BlockSpec(memory_space=pl.ANY)


def params(mib):
    return pltpu.CompilerParams(vmem_limit_bytes=mib << 20)


def cost(flops, bytes_accessed):
    return pl.CostEstimate(flops=flops, bytes_accessed=bytes_accessed, transcendentals=0)


def shift(value, axis, step):
    n = lax.axis_size(axis)
    return lax.ppermute(value, axis, [(i, (i + step) % n) for i in range(n)])


def swap(value, axis):
    return shift(value, axis, 1)


def relative(blocks, x, l):
    turned = lax.dynamic_slice_in_dim(jnp.concatenate([blocks, blocks], 0), x, X, 0)
    return jnp.where(l == 0, turned, turned[:, ::-1])


def after(values, *others):
    return lax.optimization_barrier((values, *others))[0]


def add(*values):
    total = values[0].astype(F32)
    for value in values[1:]:
        total = total + value.astype(F32)
    return total


def normed_kernel(z_ref, check_ref, gain_ref, out_ref, normed_ref):
    local, width = check_ref.shape
    span = width // (H * Z * C)
    fine = span // T
    per = 128 // fine
    values = check_ref[...].astype(F32)
    inv_rms = lax.rsqrt(jnp.mean(values * values, axis=1, keepdims=True) + 1e-05)
    normed_ref[...] = (values * inv_rms * gain_ref[...].astype(F32)).astype(BF)
    groups = Z * H // per
    lines = []
    for c in range(C):
        for group in range(groups):
            pieces = []
            for piece in range(per):
                k, h = divmod(group * per + piece, H)
                at = ((h * Z + lax.rem(z_ref[0] + k, Z)) * C + c) * span
                pieces.append(normed_ref[:, pl.ds(pl.multiple_of(at, span), span)])
            lines.append(jnp.concatenate(pieces, axis=1))
    stacked = jnp.concatenate(lines, axis=0)
    size = per * span
    row = lax.broadcasted_iota(jnp.int32, (size, size), 0)
    column = lax.broadcasted_iota(jnp.int32, (size, size), 1)
    k, t, i = row // span, (row // fine) % T, row % fine
    places = jnp.where(column == t * 128 + k * fine + i, 1.0, 0.0).astype(BF)
    placed = jnp.dot(stacked, places, preferred_element_type=F32).astype(BF)
    for c in range(C):
        for group in range(groups):
            at = (c * groups + group) * local
            for t in range(T):
                out_ref[c * T + t, :, group * 128 : (group + 1) * 128] = placed[
                    at : at + local, t * 128 : (t + 1) * 128
                ]


def normed_parts(z, checkpoint, gain):
    local, width = checkpoint.shape
    return pl.pallas_call(
        normed_kernel,
        in_specs=[SMEM, VMEM, VMEM],
        out_specs=VMEM,
        out_shape=jax.ShapeDtypeStruct((C * T, local, width // (C * T)), BF),
        scratch_shapes=[pltpu.VMEM((local, width), BF)],
        compiler_params=params(20),
        cost_estimate=cost(2 * local * width * 1024, 4 * local * width),
    )(z.reshape(1), checkpoint, gain)


KEPT = ((0, 0), (0, 1), (1, 0), (3, 1))
SENT = ((2, 0), (2, 1), (1, 1), (3, 0))


def terms_kernel(cot_ref, w_ref, *refs):
    kept, token = refs[-T // 2 - 2 : -T // 2]
    sent = refs[-T // 2 :]
    token[...] = jnp.zeros(token.shape, F32)
    product = lax.dot_general(
        cot_ref[...], w_ref[...], (((1,), (1,)), ((), ())), preferred_element_type=F32
    )
    rows = product.shape[0] // T
    block = lambda dx, dl: product[(dx * L + dl) * rows :][:rows].astype(BF)
    for i, key in enumerate(KEPT):
        kept[i] = block(*key)
    for key, out in zip(SENT, sent):
        out[...] = block(*key)


def grad_terms(cot, weight, *tokens, tile=2048):
    rows, depth = cot.shape
    width = weight.shape[0]
    own = rows // T
    outs = pl.pallas_call(
        terms_kernel,
        grid=(width // tile,),
        in_specs=[
            pl.BlockSpec((rows, depth), lambda i: (0, 0)),
            pl.BlockSpec((tile, depth), lambda i: (i, 0)),
        ]
        + [ANY] * len(tokens),
        out_specs=[
            pl.BlockSpec((len(KEPT), own, tile), lambda i: (0, 0, i)),
            pl.BlockSpec((8, 128), lambda i: (0, 0)),
        ]
        + [pl.BlockSpec((own, tile), lambda i: (0, i))] * len(SENT),
        out_shape=[
            jax.ShapeDtypeStruct((len(KEPT), own, width), BF),
            jax.ShapeDtypeStruct((8, 128), F32),
        ]
        + [jax.ShapeDtypeStruct((own, width), BF)] * len(SENT),
        compiler_params=params(58),
        cost_estimate=cost(
            4 * rows * depth * width, 2 * (rows * depth + width * depth + rows * width)
        ),
    )(cot, weight, *tokens)
    return outs[0], outs[1], outs[2:]


def weight_kernel(scale, count, sent, core_ref, left_ref, *refs):
    kept, turned = refs[-len(sent) - 2], refs[-1]
    outs = refs[-len(sent) - 1 : -1]
    tokens = left_ref.shape[1]

    @pl.when(pl.program_id(0) == 0)
    def _():
        turned[:, :tokens] = left_ref[core_ref[0]].T
        turned[:, tokens:] = left_ref[1 - core_ref[0]].T

    for i in range(count):

        @pl.when(pl.program_id(0) == i)
        def _():
            right = jnp.concatenate([refs[i][...], refs[count + i][...]], axis=0)
            product = jnp.dot(turned[...], right, preferred_element_type=F32)
            product = (product * scale).astype(BF)
            kept[...] = product.reshape(kept.shape)
            rows = product.shape[0] // Z
            for k, out in zip(sent, outs):
                out[...] = product[k * rows : (k + 1) * rows].reshape(out.shape)


def weight_terms(core, left, own, other, scale, sent, *tokens):
    cores, rows, features = left.shape
    columns = own[0].shape[1]
    count = len(own)
    fine = features // (Z * H)
    whole = lambda shape: pl.BlockSpec(shape, lambda i: (0,) * len(shape))
    return pl.pallas_call(
        functools.partial(weight_kernel, scale, count, sent),
        grid=(count,),
        in_specs=[SMEM, whole(left.shape)]
        + [whole(own[0].shape)] * (2 * count)
        + [ANY] * len(tokens),
        out_specs=[pl.BlockSpec((Z, H, 1, fine, columns), lambda i: (0, 0, i, 0, 0))]
        + [pl.BlockSpec((H, 1, fine, columns), lambda i: (0, i, 0, 0))] * len(sent),
        out_shape=[jax.ShapeDtypeStruct((Z, H, count, fine, columns), BF)]
        + [jax.ShapeDtypeStruct((H, count, fine, columns), BF)] * len(sent),
        scratch_shapes=[pltpu.VMEM((features, cores * rows), BF)],
        compiler_params=params(58),
        cost_estimate=cost(
            2 * features * cores * rows * columns * count,
            2 * (features * cores * rows + (cores * rows + features) * columns * count),
        ),
    )(core.reshape(1), left, *own, *other, *tokens)


def sums_kernel(groups, *refs):
    count = len(groups)
    outs, held, done = (refs[len(refs) - i * count :][:count] for i in (3, 2, 1))
    at, copies, others = 0, [], []
    for (index, size), buffer, semaphore in zip(groups, held, done):
        copies.append(pltpu.make_async_copy(refs[at].at[index], buffer, semaphore))
        copies[-1].start()
        others.append(refs[at + 1 : at + size])
        at += size
    for copy, buffer, other, out in zip(copies, held, others, outs):
        copy.wait()
        out[...] = add(buffer[...], *[ref[...] for ref in other]).astype(BF)


def sums(groups, *tokens):
    shape = groups[0][2].shape
    specs, values = [], []
    for stack, _, *arrays in groups:
        specs += [ANY] + [VMEM] * len(arrays)
        values += [stack] + arrays
    return pl.pallas_call(
        functools.partial(sums_kernel, [(group[1], len(group) - 1) for group in groups]),
        in_specs=specs + [ANY] * len(tokens),
        out_specs=[VMEM] * len(groups),
        out_shape=[jax.ShapeDtypeStruct(shape, BF) for group in groups],
        scratch_shapes=[pltpu.VMEM(shape, BF)] * len(groups)
        + [pltpu.SemaphoreType.DMA(())] * len(groups),
        compiler_params=params(12),
        cost_estimate=cost(8 * math.prod(shape), 16 * math.prod(shape)),
    )(*values, *tokens)


def input_kernel(check_ref, gain_ref, kept_ref, *refs):
    out_ref = refs[-1]
    values = check_ref[...].astype(F32)
    inv_rms = lax.rsqrt(jnp.mean(values * values, axis=1, keepdims=True) + 1e-05)
    unit_rows = values * inv_rms
    scaled = add(kept_ref[0], *[ref[...] for ref in refs[:3]]) * gain_ref[...].astype(F32)
    mean = jnp.mean(scaled * unit_rows, axis=1, keepdims=True)
    out_ref[...] = (inv_rms * (scaled - unit_rows * mean)).astype(BF)


def input_out(checkpoint, gain, kept, parts, *tokens, rows=16):
    local, width = checkpoint.shape
    spec = pl.BlockSpec((rows, width), lambda i: (i, 0))
    return pl.pallas_call(
        input_kernel,
        grid=(local // rows,),
        in_specs=[
            spec,
            pl.BlockSpec((1, width), lambda i: (0, 0)),
            pl.BlockSpec((1, rows, width), lambda i: (0, i, 0)),
        ]
        + [spec] * len(parts)
        + [ANY] * len(tokens),
        out_specs=spec,
        out_shape=jax.ShapeDtypeStruct((local, width), BF),
        compiler_params=params(16),
        cost_estimate=cost(12 * local * width, 12 * local * width),
    )(checkpoint, gain, kept, *parts, *tokens)


def blocks_kernel(order_ref, weight_ref, *refs):
    out_ref, held, done = refs[-3:]
    columns = weight_ref.shape[-1]
    fine = weight_ref.shape[2]
    count = T // 2
    copies = [
        pltpu.make_async_copy(refs[3 * half].at[0], held.at[half], done.at[half]) for half in range(2)
    ]
    for copy in copies:
        copy.start()
    for copy in copies:
        copy.wait()
    dots = [jnp.zeros((fine, 1), F32) for _ in range(H)]
    for i in range(T):
        half = i // count
        terms = (held.at[half],) + tuple(refs[3 * half + 1 : 3 * half + 3])
        t = order_ref[i]
        for h in range(H):
            value = add(*[term[h, i % count] for term in terms]).astype(BF)
            out_ref[h * T + t, :, :columns] = value
            product = value.astype(F32) * weight_ref[t, h].astype(F32)
            dots[h] += jnp.sum(product, axis=1, keepdims=True)
    lane = lax.broadcasted_iota(jnp.int32, (fine, 128), 1)
    for h in range(H):
        high = dots[h].astype(BF).astype(F32)
        extra = jnp.where(lane == 0, high, jnp.where(lane == 1, dots[h] - high, 0.0)).astype(BF)
        for t in range(T):
            out_ref[h * T + t, :, columns:] = extra


def last_blocks(order, weight, terms, *tokens):
    fine, columns = weight.shape[2:]
    return pl.pallas_call(
        blocks_kernel,
        in_specs=[SMEM, VMEM] + [ANY, VMEM, VMEM] * 2 + [ANY] * len(tokens),
        out_specs=VMEM,
        out_shape=jax.ShapeDtypeStruct((H * T, fine, columns + 128), BF),
        scratch_shapes=[
            pltpu.VMEM((2,) + terms[1].shape, BF),
            pltpu.SemaphoreType.DMA((2,)),
        ],
        compiler_params=params(12),
        cost_estimate=cost(5 << 20, 5 << 20),
    )(order, weight, *terms, *tokens)


def finish_kernel(group_ref, gain_ref, blocks_ref, weight_ref, gain_out_ref):
    columns = weight_ref.shape[1]
    fine = blocks_ref.shape[1]
    lane = lax.broadcasted_iota(jnp.int32, (8, 128), 1)
    pick = jnp.where(lane < 2, 1.0, 0.0).astype(BF)
    dots = jnp.zeros((8, weight_ref.shape[0]), F32)
    for h in range(H):
        extra = blocks_ref[h * T : (h + 1) * T, :, columns:].reshape(T * fine, 128)
        dots += lax.dot_general(pick, extra, (((1,), (1,)), ((), ())), preferred_element_type=F32)
    gain_out_ref[...] = dots[:1] / gain_ref[pl.ds(group_ref[0], 1), :].astype(F32)
    for t in range(T):
        weight_ref[t * fine : (t + 1) * fine] = add(
            *[blocks_ref[h * T + t, :, :columns] for h in range(H)]
        )


def finish(group, gain, blocks):
    fine, width = blocks.shape[1:]
    rows = T * fine
    weight, gain_row = pl.pallas_call(
        finish_kernel,
        in_specs=[SMEM, VMEM, VMEM],
        out_specs=[VMEM, VMEM],
        out_shape=[
            jax.ShapeDtypeStruct((rows, width - 128), F32),
            jax.ShapeDtypeStruct((1, rows), F32),
        ],
        compiler_params=params(8),
        cost_estimate=cost(5 << 20, 5 << 20),
    )(group.reshape(1), gain.astype(F32).reshape(-1, rows), blocks)
    return weight, gain_row.reshape(rows)


def shards(checkpoint, gain, qkv_weight, qkv_cot):
    h, z, c = lax.axis_index("h"), lax.axis_index("z"), lax.axis_index("c")
    x, l = lax.axis_index("x"), lax.axis_index("l")
    local, width = checkpoint.shape
    tokens, columns = qkv_cot.shape
    grad_scale = 1.0 / math.sqrt(tokens * H * Z * C)
    fine = width // (H * Z * C * T)
    gain_row = gain.reshape(1, width)

    with jax.named_scope("normed_exchange"):
        parts = normed_parts(z, checkpoint, gain_row)
        left = lax.all_to_all(parts, ("c",) + TENSOR, 0, 0, tiled=True)
        left = left.reshape(C, tokens, Z * H * fine)

    near = {(0, 0): qkv_cot}
    with jax.named_scope("cot_gather"):
        near[0, 1] = swap(qkv_cot, "l")
        for step in (1, 3, 2):
            near[step, 0] = shift(qkv_cot, "x", -step)

    with jax.named_scope("input_terms"):
        cot_near = relative(qkv_cot.reshape(X, L, local, columns), x, l)
        kept, multiplied, sent = grad_terms(cot_near.reshape(tokens, columns), qkv_weight, parts)

    keys = (((0, 0), (0, 1), (1, 0), (3, 0)), ((2, 0), (1, 1), (3, 1), (2, 1)))
    across = {(0, 0): swap(qkv_cot, "c")}

    def product(some, going, *given):
        own, other = [near[key] for key in some], [across[key] for key in some]
        return weight_terms(c, left, own, other, grad_scale, going, *given)

    with jax.named_scope("cot_gather"):
        for key in ((0, 1), (1, 0), (3, 0), (2, 0)):
            near[key] = after(near[key], multiplied, left)
        near[3, 1] = shift(near[0, 1], "x", 1)
        near[1, 1] = shift(near[0, 1], "x", -1)
        near[2, 1] = swap(near[2, 0], "l")
        for key in keys[0][1:]:
            across[key] = swap(near[key], "c")
    with jax.named_scope("weight_terms"):
        a, a_4, a_5 = product(keys[0], (4, 5), multiplied)
    with jax.named_scope("cot_gather"):
        for key in keys[1]:
            near[key] = after(near[key], a_4)
            across[key] = swap(near[key], "c")
    with jax.named_scope("weight_terms"):
        b, b_3, b_4 = product(keys[1], (3, 4), a_4)

    with jax.named_scope("chains"):
        up = lambda value: shift(value, "z", 1)
        down = lambda value: shift(value, "z", -1)
        sent = dict(zip(SENT, after(sent, near[1, 1], near[3, 1])))
        up_a, down_a = up(a_4), down(a_5)
        far_up, far_down = shift(sent[2, 0], "x", 1), shift(sent[2, 1], "x", -1)
        up_1 = shift(sent[1, 1], "x", 1)
        up_b, down_b = up(b_3), down(b_4)
        s1 = sums([(a, 3, up_a), (a, 6, down_a)], b_3)
        up_a, down_a = up(s1[0]), down(s1[1])
        s2 = sums([(kept, 3, far_down), (kept, 2, far_up)], s1[0])
        down_1, up_0 = shift(s2[0], "x", -1), shift(s2[1], "x", 1)
        down_0 = shift(after(sent[3, 0], s2[0]), "x", -1)
        s3 = sums([(b, 2, up_b), (b, 5, down_b)], s2[0])
        up_b, down_b = up(s3[0]), down(s3[1])
        s4 = sums([(a, 2, up_a), (a, 7, down_a)], s3[0])
        up_a, down_a = up(s4[0]), down(s4[1])
        s5 = sums([(b, 1, up_b), (b, 6, down_b)], s4[0])
        up_b, down_b = up(s5[0]), down(s5[1])
        s6 = sums([(kept, 1, up_1, down_1)], s5[0])
        other_l = swap(s6[0], "l")
        s7 = sums([(a, 1, up_a)], s6[0])
        up_a = up(s7[0])
        s8 = sums([(b, 7, down_b)], s7[0], up_0, down_0)
        down_b = down(s8[0])

    with jax.named_scope("weight_rows"):
        mine = qkv_weight.reshape(H, Z, C, T, fine, columns)
        mine = lax.dynamic_slice(mine, (0, z, c, 0, 0, 0), (H, 1, 1, T, fine, columns))
        mine = after(mine.reshape(H, T, fine, columns), s3[0])
        mine = lax.all_to_all(mine.swapaxes(0, 1), TENSOR, 0, 0, tiled=True)

    with jax.named_scope("input_out"):
        input_grad = input_out(checkpoint, gain_row, kept, (up_0, down_0, other_l), s8[0])

    with jax.named_scope("weight_out"):
        order = jnp.stack(
            [lax.rem(x + i, X) * L + lax.rem(l + j, L) for some in keys for i, j in some]
        )
        blocks = last_blocks(order, mine, (a, up_a, down_a, b, up_b, down_b), other_l)
        blocks = lax.all_to_all(blocks, ("h",) + TENSOR, 0, 0, tiled=True)
        weight_out, gain_out = finish((h * Z + z) * C + c, gain, blocks)
    return (input_grad, gain_out, weight_out)


def solution(mesh):
    fine_mesh = Mesh(mesh.devices.reshape(H, Z, C, X, L), DP + TENSOR)
    rows = P(DP + TENSOR, None)
    in_specs = (rows, P(), P(None, TENSOR), P(DP, TENSOR))
    out_specs = (rows, P(DP), P(DP, TENSOR))
    return jax.shard_map(
        shards, mesh=fine_mesh, in_specs=in_specs, out_specs=out_specs, check_vma=False
    )
```

```python
import functools
import math

import jax
import jax.numpy as jnp
from jax import lax
from jax.experimental import pallas as pl
from jax.experimental.pallas import tpu as pltpu
from jax.sharding import Mesh
from jax.sharding import PartitionSpec as P

H, Z, C, X, L = 2, 8, 2, 4, 2
T = X * L
DP = ("h", "z", "c")
TENSOR = ("x", "l")
BF = jnp.bfloat16
F32 = jnp.float32

VMEM = pl.BlockSpec(memory_space=pltpu.VMEM)
SMEM = pl.BlockSpec(memory_space=pltpu.SMEM)
ANY = pl.BlockSpec(memory_space=pl.ANY)


def params(mib):
    return pltpu.CompilerParams(vmem_limit_bytes=mib << 20)


def cost(flops, bytes_accessed):
    return pl.CostEstimate(flops=flops, bytes_accessed=bytes_accessed, transcendentals=0)


SMALL = cost(1000, 1000)


def shift(value, axis, step):
    n = lax.axis_size(axis)
    return lax.ppermute(value, axis, [(i, (i + step) % n) for i in range(n)])


def swap(value, axis):
    return shift(value, axis, 1)


def relative(blocks, x, l):
    turned = lax.dynamic_slice_in_dim(jnp.concatenate([blocks, blocks], 0), x, X, 0)
    return jnp.where(l == 0, turned, turned[:, ::-1])


def after(values, *others):
    return lax.optimization_barrier((values, *others))[0]


def add(*values):
    total = values[0].astype(F32)
    for value in values[1:]:
        total = total + value.astype(F32)
    return total


def normed_kernel(z_ref, check_ref, gain_ref, out_ref, normed_ref):
    local, width = check_ref.shape
    span = width // (H * Z * C)
    fine = span // T
    per = 128 // fine
    values = check_ref[...].astype(F32)
    inv_rms = lax.rsqrt(jnp.mean(values * values, axis=1, keepdims=True) + 1e-05)
    normed_ref[...] = (values * inv_rms * gain_ref[...].astype(F32)).astype(BF)
    groups = Z * H // per
    lines = []
    for c in range(C):
        for group in range(groups):
            pieces = []
            for piece in range(per):
                k, h = divmod(group * per + piece, H)
                at = ((h * Z + lax.rem(z_ref[0] + k, Z)) * C + c) * span
                pieces.append(normed_ref[:, pl.ds(pl.multiple_of(at, span), span)])
            lines.append(jnp.concatenate(pieces, axis=1))
    stacked = jnp.concatenate(lines, axis=0)
    size = per * span
    row = lax.broadcasted_iota(jnp.int32, (size, size), 0)
    column = lax.broadcasted_iota(jnp.int32, (size, size), 1)
    k, t, i = row // span, (row // fine) % T, row % fine
    places = jnp.where(column == t * 128 + k * fine + i, 1.0, 0.0).astype(BF)
    placed = jnp.dot(stacked, places, preferred_element_type=F32).astype(BF)
    for c in range(C):
        for group in range(groups):
            at = (c * groups + group) * local
            for t in range(T):
                out_ref[c * T + t, :, group * 128 : (group + 1) * 128] = placed[
                    at : at + local, t * 128 : (t + 1) * 128
                ]


def normed_parts(z, checkpoint, gain):
    local, width = checkpoint.shape
    return pl.pallas_call(
        normed_kernel,
        in_specs=[SMEM, VMEM, VMEM],
        out_specs=VMEM,
        out_shape=jax.ShapeDtypeStruct((C * T, local, width // (C * T)), BF),
        scratch_shapes=[pltpu.VMEM((local, width), BF)],
        compiler_params=params(20),
        cost_estimate=cost(2 * local * width * 1024, 4 * local * width),
    )(z.reshape(1), checkpoint, gain)


KEPT = ((0, 0), (0, 1), (1, 0), (1, 1), (3, 0), (3, 1))
SENT = ((2, 0), (2, 1))


def terms_kernel(cot_ref, w_ref, *refs):
    kept, token, *sent = refs[-len(SENT) - 2 :]
    token[...] = jnp.zeros(token.shape, F32)
    product = lax.dot_general(
        cot_ref[...], w_ref[...], (((1,), (1,)), ((), ())), preferred_element_type=F32
    )
    rows = product.shape[0] // T
    block = lambda dx, dl: product[(dx * L + dl) * rows :][:rows].astype(BF)
    for i, key in enumerate(KEPT):
        kept[i] = block(*key)
    for key, out in zip(SENT, sent):
        out[...] = block(*key)


def grad_terms(cot, weight, *tokens, tile=2048):
    rows, depth = cot.shape
    width = weight.shape[0]
    own = rows // T
    outs = pl.pallas_call(
        terms_kernel,
        grid=(width // tile,),
        in_specs=[
            pl.BlockSpec((rows, depth), lambda i: (0, 0)),
            pl.BlockSpec((tile, depth), lambda i: (i, 0)),
        ]
        + [ANY] * len(tokens),
        out_specs=[
            pl.BlockSpec((len(KEPT), own, tile), lambda i: (0, 0, i)),
            pl.BlockSpec((8, 128), lambda i: (0, 0)),
        ]
        + [pl.BlockSpec((own, tile), lambda i: (0, i))] * len(SENT),
        out_shape=[
            jax.ShapeDtypeStruct((len(KEPT), own, width), BF),
            jax.ShapeDtypeStruct((8, 128), F32),
        ]
        + [jax.ShapeDtypeStruct((own, width), BF)] * len(SENT),
        compiler_params=params(58),
        cost_estimate=cost(
            4 * rows * depth * width, 2 * (rows * depth + width * depth + rows * width)
        ),
    )(cot, weight, *tokens)
    return outs[0], outs[1], outs[2:]


def weight_kernel(scale, count, sent, core_ref, left_ref, *refs):
    kept, turned = refs[-len(sent) - 2], refs[-1]
    outs = refs[-len(sent) - 1 : -1]
    tokens = left_ref.shape[1]

    @pl.when(pl.program_id(0) == 0)
    def _():
        turned[:, :tokens] = left_ref[core_ref[0]].T
        turned[:, tokens:] = left_ref[1 - core_ref[0]].T

    for i in range(count):

        @pl.when(pl.program_id(0) == i)
        def _():
            right = jnp.concatenate([refs[i][...], refs[count + i][...]], axis=0)
            product = jnp.dot(turned[...], right, preferred_element_type=F32)
            product = (product * scale).astype(BF)
            kept[...] = product.reshape(kept.shape)
            rows = product.shape[0] // Z
            for k, out in zip(sent, outs):
                out[...] = product[k * rows : (k + 1) * rows].reshape(out.shape)


def weight_terms(core, left, own, other, scale, sent, *tokens):
    cores, rows, features = left.shape
    columns = own[0].shape[1]
    count = len(own)
    fine = features // (Z * H)
    whole = lambda shape: pl.BlockSpec(shape, lambda i: (0,) * len(shape))
    return pl.pallas_call(
        functools.partial(weight_kernel, scale, count, sent),
        grid=(count,),
        in_specs=[SMEM, whole(left.shape)]
        + [whole(own[0].shape)] * (2 * count)
        + [ANY] * len(tokens),
        out_specs=[pl.BlockSpec((Z, H, 1, fine, columns), lambda i: (0, 0, i, 0, 0))]
        + [pl.BlockSpec((H, 1, fine, columns), lambda i: (0, i, 0, 0))] * len(sent),
        out_shape=[jax.ShapeDtypeStruct((Z, H, count, fine, columns), BF)]
        + [jax.ShapeDtypeStruct((H, count, fine, columns), BF)] * len(sent),
        scratch_shapes=[pltpu.VMEM((features, cores * rows), BF)],
        compiler_params=params(58),
        cost_estimate=SMALL,
    )(core.reshape(1), left, *own, *other, *tokens)


def sums_kernel(groups, *refs):
    count = len(groups)
    outs, held, done = (refs[len(refs) - i * count :][:count] for i in (3, 2, 1))
    at, copies, others = 0, [], []
    for (index, size), buffer, semaphore in zip(groups, held, done):
        copies.append(pltpu.make_async_copy(refs[at].at[index], buffer, semaphore))
        copies[-1].start()
        others.append(refs[at + 1 : at + size])
        at += size
    for copy, buffer, other, out in zip(copies, held, others, outs):
        copy.wait()
        out[...] = add(buffer[...], *[ref[...] for ref in other]).astype(BF)


def sums(groups, *tokens):
    shape = groups[0][2].shape
    specs, values = [], []
    for stack, _, *arrays in groups:
        specs += [ANY] + [VMEM] * len(arrays)
        values += [stack] + arrays
    return pl.pallas_call(
        functools.partial(sums_kernel, [(group[1], len(group) - 1) for group in groups]),
        in_specs=specs + [ANY] * len(tokens),
        out_specs=[VMEM] * len(groups),
        out_shape=[jax.ShapeDtypeStruct(shape, BF) for group in groups],
        scratch_shapes=[pltpu.VMEM(shape, BF)] * len(groups)
        + [pltpu.SemaphoreType.DMA(())] * len(groups),
        compiler_params=params(12),
        cost_estimate=SMALL,
    )(*values, *tokens)


def step_kernel(kept_ref, up_ref, down_ref, *refs):
    up_out, down_out = refs[-2:]
    up_out[0] = add(kept_ref[2], up_ref[...]).astype(BF)
    up_out[1] = kept_ref[3]
    down_out[0] = kept_ref[4]
    down_out[1] = add(kept_ref[5], down_ref[...]).astype(BF)


def next_step(kept, far_up, far_down, *tokens, tile=2048):
    count, own, width = kept.shape
    spec = pl.BlockSpec((own, tile), lambda i: (0, i))
    pair = pl.BlockSpec((2, own, tile), lambda i: (0, 0, i))
    return pl.pallas_call(
        step_kernel,
        grid=(width // tile,),
        in_specs=[pl.BlockSpec((count, own, tile), lambda i: (0, 0, i)), spec, spec]
        + [ANY] * len(tokens),
        out_specs=[pair, pair],
        out_shape=[jax.ShapeDtypeStruct((2, own, width), BF)] * 2,
        compiler_params=params(58),
        cost_estimate=SMALL,
    )(kept, far_up, far_down, *tokens)


def other_kernel(kept_ref, up_ref, down_ref, *refs):
    refs[-1][...] = add(kept_ref[0], up_ref[0], down_ref[0]).astype(BF)


def for_other(kept, up, down, *tokens, tile=2048):
    _, own, width = kept.shape
    spec = pl.BlockSpec((1, own, tile), lambda i: (1, 0, i))
    return pl.pallas_call(
        other_kernel,
        grid=(width // tile,),
        in_specs=[spec] * 3 + [ANY] * len(tokens),
        out_specs=pl.BlockSpec((own, tile), lambda i: (0, i)),
        out_shape=jax.ShapeDtypeStruct((own, width), BF),
        compiler_params=params(58),
        cost_estimate=SMALL,
    )(kept, up, down, *tokens)


def input_kernel(check_ref, gain_ref, kept_ref, *refs):
    out_ref = refs[-1]
    values = check_ref[...].astype(F32)
    inv_rms = lax.rsqrt(jnp.mean(values * values, axis=1, keepdims=True) + 1e-05)
    unit_rows = values * inv_rms
    scaled = add(kept_ref[0], refs[0][0], refs[1][0], refs[2][...]) * gain_ref[...].astype(F32)
    mean = jnp.mean(scaled * unit_rows, axis=1, keepdims=True)
    out_ref[...] = (inv_rms * (scaled - unit_rows * mean)).astype(BF)


def input_out(checkpoint, gain, kept, up, down, other_l, *tokens, rows=16):
    local, width = checkpoint.shape
    spec = pl.BlockSpec((rows, width), lambda i: (i, 0))
    first = pl.BlockSpec((1, rows, width), lambda i: (0, i, 0))
    return pl.pallas_call(
        input_kernel,
        grid=(local // rows,),
        in_specs=[spec, pl.BlockSpec((1, width), lambda i: (0, 0)), first, first, first, spec]
        + [ANY] * len(tokens),
        out_specs=spec,
        out_shape=jax.ShapeDtypeStruct((local, width), BF),
        compiler_params=params(58),
        cost_estimate=SMALL,
    )(checkpoint, gain, kept, up, down, other_l, *tokens)


def blocks_kernel(order_ref, weight_ref, *refs):
    out_ref, held, done = refs[-3:]
    columns = weight_ref.shape[-1]
    fine = weight_ref.shape[2]
    count = T // 2
    copies = [
        pltpu.make_async_copy(refs[3 * half].at[0], held.at[half], done.at[half]) for half in range(2)
    ]
    for copy in copies:
        copy.start()
    for copy in copies:
        copy.wait()
    dots = [jnp.zeros((fine, 1), F32) for _ in range(H)]
    for i in range(T):
        half = i // count
        terms = (held.at[half],) + tuple(refs[3 * half + 1 : 3 * half + 3])
        t = order_ref[i]
        for h in range(H):
            value = add(*[term[h, i % count] for term in terms]).astype(BF)
            out_ref[h * T + t, :, :columns] = value
            product = value.astype(F32) * weight_ref[t, h].astype(F32)
            dots[h] += jnp.sum(product, axis=1, keepdims=True)
    lane = lax.broadcasted_iota(jnp.int32, (fine, 128), 1)
    for h in range(H):
        high = dots[h].astype(BF).astype(F32)
        extra = jnp.where(lane == 0, high, jnp.where(lane == 1, dots[h] - high, 0.0)).astype(BF)
        for t in range(T):
            out_ref[h * T + t, :, columns:] = extra


def last_blocks(order, weight, terms, *tokens):
    fine, columns = weight.shape[2:]
    return pl.pallas_call(
        blocks_kernel,
        in_specs=[SMEM, VMEM] + [ANY, VMEM, VMEM] * 2 + [ANY] * len(tokens),
        out_specs=VMEM,
        out_shape=jax.ShapeDtypeStruct((H * T, fine, columns + 128), BF),
        scratch_shapes=[
            pltpu.VMEM((2,) + terms[1].shape, BF),
            pltpu.SemaphoreType.DMA((2,)),
        ],
        compiler_params=params(12),
        cost_estimate=SMALL,
    )(order, weight, *terms, *tokens)


def finish_kernel(group_ref, gain_ref, blocks_ref, weight_ref, gain_out_ref):
    columns = weight_ref.shape[1]
    fine = blocks_ref.shape[1]
    lane = lax.broadcasted_iota(jnp.int32, (8, 128), 1)
    pick = jnp.where(lane < 2, 1.0, 0.0).astype(BF)
    dots = jnp.zeros((8, weight_ref.shape[0]), F32)
    for h in range(H):
        extra = blocks_ref[h * T : (h + 1) * T, :, columns:].reshape(T * fine, 128)
        dots += lax.dot_general(pick, extra, (((1,), (1,)), ((), ())), preferred_element_type=F32)
    gain_out_ref[...] = dots[:1] / gain_ref[pl.ds(group_ref[0], 1), :].astype(F32)
    for t in range(T):
        weight_ref[t * fine : (t + 1) * fine] = add(
            *[blocks_ref[h * T + t, :, :columns] for h in range(H)]
        )


def finish(group, gain, blocks):
    fine, width = blocks.shape[1:]
    rows = T * fine
    weight, gain_row = pl.pallas_call(
        finish_kernel,
        in_specs=[SMEM, VMEM, VMEM],
        out_specs=[VMEM, VMEM],
        out_shape=[
            jax.ShapeDtypeStruct((rows, width - 128), F32),
            jax.ShapeDtypeStruct((1, rows), F32),
        ],
        compiler_params=params(8),
        cost_estimate=SMALL,
    )(group.reshape(1), gain.astype(F32).reshape(-1, rows), blocks)
    return weight, gain_row.reshape(rows)


def shards(checkpoint, gain, qkv_weight, qkv_cot):
    h, z, c = lax.axis_index("h"), lax.axis_index("z"), lax.axis_index("c")
    x, l = lax.axis_index("x"), lax.axis_index("l")
    local, width = checkpoint.shape
    tokens, columns = qkv_cot.shape
    grad_scale = 1.0 / math.sqrt(tokens * H * Z * C)
    fine = width // (H * Z * C * T)
    gain_row = gain.reshape(1, width)

    with jax.named_scope("normed_exchange"):
        parts = normed_parts(z, checkpoint, gain_row)
        left = lax.all_to_all(parts, ("c",) + TENSOR, 0, 0, tiled=True)
        left = left.reshape(C, tokens, Z * H * fine)

    near = {(0, 0): qkv_cot}
    with jax.named_scope("cot_gather"):
        near[0, 1] = swap(qkv_cot, "l")
        for step in (1, 3):
            near[step, 0] = shift(qkv_cot, "x", -step)

    with jax.named_scope("input_terms"):
        cot_near = relative(qkv_cot.reshape(X, L, local, columns), x, l)
        kept, multiplied, sent = grad_terms(cot_near.reshape(tokens, columns), qkv_weight, parts)

    keys = (((0, 0), (0, 1), (1, 0), (3, 0)), ((2, 0), (1, 1), (3, 1), (2, 1)))
    across = {(0, 0): swap(after(qkv_cot, parts), "c")}

    def product(some, going, *given):
        own, other = [near[key] for key in some], [across[key] for key in some]
        return weight_terms(c, left, own, other, grad_scale, going, *given)

    with jax.named_scope("cot_gather"):
        near[2, 0] = shift(after(qkv_cot, multiplied), "x", -2)
        for key in ((0, 1), (1, 0), (3, 0)):
            near[key] = after(near[key], multiplied, left)
        near[3, 1] = shift(near[0, 1], "x", 1)
        near[1, 1] = shift(near[0, 1], "x", -1)
        near[2, 1] = swap(near[2, 0], "l")
        for key in keys[0][1:]:
            across[key] = swap(near[key], "c")
    with jax.named_scope("input_step"):
        far_up, far_down = shift(sent[0], "x", 1), shift(sent[1], "x", -1)
    with jax.named_scope("weight_terms"):
        a, a_4, a_5 = product(keys[0], (4, 5), multiplied)
    with jax.named_scope("input_step"):
        x_up, x_down = next_step(kept, far_up, far_down, a_4)
        up_x, down_x = shift(x_up, "x", 1), shift(x_down, "x", -1)
    with jax.named_scope("cot_gather"):
        for key in keys[1]:
            near[key] = after(near[key], a_4)
            across[key] = swap(near[key], "c")
    with jax.named_scope("weight_terms"):
        b, b_3, b_4 = product(keys[1], (3, 4), x_up)

    with jax.named_scope("chains"):
        up = lambda value: shift(value, "z", 1)
        down = lambda value: shift(value, "z", -1)
        up_a, down_a = up(a_4), down(a_5)
        up_b, down_b = up(b_3), down(b_4)
        s1 = sums([(a, 3, up_a), (a, 6, down_a)], b_3)
        up_a, down_a = up(s1[0]), down(s1[1])
        s3 = sums([(b, 2, up_b), (b, 5, down_b)], s1[0])
        up_b, down_b = up(s3[0]), down(s3[1])
        s4 = sums([(a, 2, up_a), (a, 7, down_a)], s3[0])
        up_a, down_a = up(s4[0]), down(s4[1])
        other_l = swap(for_other(kept, up_x, down_x, s4[0]), "l")
        s5 = sums([(b, 1, up_b), (b, 6, down_b)], s4[0])
        up_b, down_b = up(s5[0]), down(s5[1])
        s7 = sums([(a, 1, up_a)], s5[0])
        up_a = up(s7[0])
        s8 = sums([(b, 7, down_b)], s7[0])
        down_b = down(s8[0])

    with jax.named_scope("weight_rows"):
        mine = qkv_weight.reshape(H, Z, C, T, fine, columns)
        mine = lax.dynamic_slice(mine, (0, z, c, 0, 0, 0), (H, 1, 1, T, fine, columns))
        mine = after(mine.reshape(H, T, fine, columns), s3[0])
        mine = lax.all_to_all(mine.swapaxes(0, 1), TENSOR, 0, 0, tiled=True)

    with jax.named_scope("input_out"):
        input_grad = input_out(checkpoint, gain_row, kept, up_x, down_x, other_l, s8[0])

    with jax.named_scope("weight_out"):
        order = jnp.stack(
            [lax.rem(x + i, X) * L + lax.rem(l + j, L) for some in keys for i, j in some]
        )
        blocks = last_blocks(order, mine, (a, up_a, down_a, b, up_b, down_b), other_l)
        blocks = lax.all_to_all(blocks, ("h",) + TENSOR, 0, 0, tiled=True)
        weight_out, gain_out = finish((h * Z + z) * C + c, gain, blocks)
    return (input_grad, gain_out, weight_out)


def solution(mesh):
    fine_mesh = Mesh(mesh.devices.reshape(H, Z, C, X, L), DP + TENSOR)
    rows = P(DP + TENSOR, None)
    in_specs = (rows, P(), P(None, TENSOR), P(DP, TENSOR))
    out_specs = (rows, P(DP), P(DP, TENSOR))
    return jax.shard_map(
        shards, mesh=fine_mesh, in_specs=in_specs, out_specs=out_specs, check_vma=False
    )
```

```python
import functools
import math

import jax
import jax.numpy as jnp
from jax import lax
from jax.experimental import pallas as pl
from jax.experimental.pallas import tpu as pltpu
from jax.sharding import Mesh
from jax.sharding import PartitionSpec as P

H, Z, C, X, L = 2, 8, 2, 4, 2
T = X * L
DP = ("h", "z", "c")
TENSOR = ("x", "l")
BF = jnp.bfloat16
F32 = jnp.float32

VMEM = pl.BlockSpec(memory_space=pltpu.VMEM)
SMEM = pl.BlockSpec(memory_space=pltpu.SMEM)
ANY = pl.BlockSpec(memory_space=pl.ANY)


def params(mib):
    return pltpu.CompilerParams(vmem_limit_bytes=mib << 20)


def cost(flops, bytes_accessed):
    return pl.CostEstimate(flops=flops, bytes_accessed=bytes_accessed, transcendentals=0)


SMALL = cost(1000, 1000)


def shift(value, axis, step):
    n = lax.axis_size(axis)
    return lax.ppermute(value, axis, [(i, (i + step) % n) for i in range(n)])


def swap(value, axis):
    return shift(value, axis, 1)


def relative(blocks, x, l):
    turned = lax.dynamic_slice_in_dim(jnp.concatenate([blocks, blocks], 0), x, X, 0)
    return jnp.where(l == 0, turned, turned[:, ::-1])


def after(values, *others):
    return lax.optimization_barrier((values, *others))[0]


def add(*values):
    total = values[0].astype(F32)
    for value in values[1:]:
        total = total + value.astype(F32)
    return total


def normed_kernel(z_ref, check_ref, gain_ref, out_ref, normed_ref):
    local, width = check_ref.shape
    span = width // (H * Z * C)
    fine = span // T
    per = 128 // fine
    values = check_ref[...].astype(F32)
    inv_rms = lax.rsqrt(jnp.mean(values * values, axis=1, keepdims=True) + 1e-05)
    normed_ref[...] = (values * inv_rms * gain_ref[...].astype(F32)).astype(BF)
    groups = Z * H // per
    lines = []
    for c in range(C):
        for group in range(groups):
            pieces = []
            for piece in range(per):
                k, h = divmod(group * per + piece, H)
                at = ((h * Z + lax.rem(z_ref[0] + k, Z)) * C + c) * span
                pieces.append(normed_ref[:, pl.ds(pl.multiple_of(at, span), span)])
            lines.append(jnp.concatenate(pieces, axis=1))
    stacked = jnp.concatenate(lines, axis=0)
    size = per * span
    row = lax.broadcasted_iota(jnp.int32, (size, size), 0)
    column = lax.broadcasted_iota(jnp.int32, (size, size), 1)
    k, t, i = row // span, (row // fine) % T, row % fine
    places = jnp.where(column == t * 128 + k * fine + i, 1.0, 0.0).astype(BF)
    placed = jnp.dot(stacked, places, preferred_element_type=F32).astype(BF)
    for c in range(C):
        for group in range(groups):
            at = (c * groups + group) * local
            for t in range(T):
                out_ref[c * T + t, :, group * 128 : (group + 1) * 128] = placed[
                    at : at + local, t * 128 : (t + 1) * 128
                ]


def normed_parts(z, checkpoint, gain):
    local, width = checkpoint.shape
    return pl.pallas_call(
        normed_kernel,
        in_specs=[SMEM, VMEM, VMEM],
        out_specs=VMEM,
        out_shape=jax.ShapeDtypeStruct((C * T, local, width // (C * T)), BF),
        scratch_shapes=[pltpu.VMEM((local, width), BF)],
        compiler_params=params(20),
        cost_estimate=cost(2 * local * width * 1024, 4 * local * width),
    )(z.reshape(1), checkpoint, gain)


KEPT = ((0, 0), (0, 1), (1, 0), (3, 1))
SENT = ((2, 0), (2, 1), (1, 1), (3, 0))


def terms_kernel(cot_ref, w_ref, *refs):
    kept, token = refs[-T // 2 - 2 : -T // 2]
    sent = refs[-T // 2 :]
    token[...] = jnp.zeros(token.shape, F32)
    product = lax.dot_general(
        cot_ref[...], w_ref[...], (((1,), (1,)), ((), ())), preferred_element_type=F32
    )
    rows = product.shape[0] // T
    block = lambda dx, dl: product[(dx * L + dl) * rows :][:rows].astype(BF)
    for i, key in enumerate(KEPT):
        kept[i] = block(*key)
    for key, out in zip(SENT, sent):
        out[...] = block(*key)


def grad_terms(cot, weight, *tokens, tile=2048):
    rows, depth = cot.shape
    width = weight.shape[0]
    own = rows // T
    outs = pl.pallas_call(
        terms_kernel,
        grid=(width // tile,),
        in_specs=[
            pl.BlockSpec((rows, depth), lambda i: (0, 0)),
            pl.BlockSpec((tile, depth), lambda i: (i, 0)),
        ]
        + [ANY] * len(tokens),
        out_specs=[
            pl.BlockSpec((len(KEPT), own, tile), lambda i: (0, 0, i)),
            pl.BlockSpec((8, 128), lambda i: (0, 0)),
        ]
        + [pl.BlockSpec((own, tile), lambda i: (0, i))] * len(SENT),
        out_shape=[
            jax.ShapeDtypeStruct((len(KEPT), own, width), BF),
            jax.ShapeDtypeStruct((8, 128), F32),
        ]
        + [jax.ShapeDtypeStruct((own, width), BF)] * len(SENT),
        compiler_params=params(58),
        cost_estimate=cost(
            4 * rows * depth * width, 2 * (rows * depth + width * depth + rows * width)
        ),
    )(cot, weight, *tokens)
    return outs[0], outs[1], outs[2:]


def weight_kernel(scale, count, sent, core_ref, left_ref, *refs):
    kept, turned = refs[-len(sent) - 2], refs[-1]
    outs = refs[-len(sent) - 1 : -1]
    tokens = left_ref.shape[1]

    @pl.when(pl.program_id(0) == 0)
    def _():
        turned[:, :tokens] = left_ref[core_ref[0]].T
        turned[:, tokens:] = left_ref[1 - core_ref[0]].T

    for i in range(count):

        @pl.when(pl.program_id(0) == i)
        def _():
            right = jnp.concatenate([refs[i][...], refs[count + i][...]], axis=0)
            product = jnp.dot(turned[...], right, preferred_element_type=F32)
            product = (product * scale).astype(BF)
            kept[...] = product.reshape(kept.shape)
            rows = product.shape[0] // Z
            for k, out in zip(sent, outs):
                out[...] = product[k * rows : (k + 1) * rows].reshape(out.shape)


def weight_terms(core, left, own, other, scale, sent, *tokens):
    cores, rows, features = left.shape
    columns = own[0].shape[1]
    count = len(own)
    fine = features // (Z * H)
    whole = lambda shape: pl.BlockSpec(shape, lambda i: (0,) * len(shape))
    return pl.pallas_call(
        functools.partial(weight_kernel, scale, count, sent),
        grid=(count,),
        in_specs=[SMEM, whole(left.shape)]
        + [whole(own[0].shape)] * (2 * count)
        + [ANY] * len(tokens),
        out_specs=[pl.BlockSpec((Z, H, 1, fine, columns), lambda i: (0, 0, i, 0, 0))]
        + [pl.BlockSpec((H, 1, fine, columns), lambda i: (0, i, 0, 0))] * len(sent),
        out_shape=[jax.ShapeDtypeStruct((Z, H, count, fine, columns), BF)]
        + [jax.ShapeDtypeStruct((H, count, fine, columns), BF)] * len(sent),
        scratch_shapes=[pltpu.VMEM((features, cores * rows), BF)],
        compiler_params=params(58),
        cost_estimate=SMALL,
    )(core.reshape(1), left, *own, *other, *tokens)


def sums_kernel(groups, *refs):
    count = len(groups)
    outs, held, done = (refs[len(refs) - i * count :][:count] for i in (3, 2, 1))
    at, copies, others = 0, [], []
    for (index, size), buffer, semaphore in zip(groups, held, done):
        copies.append(pltpu.make_async_copy(refs[at].at[index], buffer, semaphore))
        copies[-1].start()
        others.append(refs[at + 1 : at + size])
        at += size
    for copy, buffer, other, out in zip(copies, held, others, outs):
        copy.wait()
        out[...] = add(buffer[...], *[ref[...] for ref in other]).astype(BF)


def sums(groups, *tokens):
    shape = groups[0][2].shape
    specs, values = [], []
    for stack, _, *arrays in groups:
        specs += [ANY] + [VMEM] * len(arrays)
        values += [stack] + arrays
    return pl.pallas_call(
        functools.partial(sums_kernel, [(group[1], len(group) - 1) for group in groups]),
        in_specs=specs + [ANY] * len(tokens),
        out_specs=[VMEM] * len(groups),
        out_shape=[jax.ShapeDtypeStruct(shape, BF) for group in groups],
        scratch_shapes=[pltpu.VMEM(shape, BF)] * len(groups)
        + [pltpu.SemaphoreType.DMA(())] * len(groups),
        compiler_params=params(12),
        cost_estimate=SMALL,
    )(*values, *tokens)


def input_kernel(check_ref, gain_ref, kept_ref, *refs):
    out_ref = refs[-1]
    values = check_ref[...].astype(F32)
    inv_rms = lax.rsqrt(jnp.mean(values * values, axis=1, keepdims=True) + 1e-05)
    unit_rows = values * inv_rms
    scaled = add(kept_ref[0], *[ref[...] for ref in refs[:3]]) * gain_ref[...].astype(F32)
    mean = jnp.mean(scaled * unit_rows, axis=1, keepdims=True)
    out_ref[...] = (inv_rms * (scaled - unit_rows * mean)).astype(BF)


def input_out(checkpoint, gain, kept, parts, *tokens, rows=16):
    local, width = checkpoint.shape
    spec = pl.BlockSpec((rows, width), lambda i: (i, 0))
    return pl.pallas_call(
        input_kernel,
        grid=(local // rows,),
        in_specs=[
            spec,
            pl.BlockSpec((1, width), lambda i: (0, 0)),
            pl.BlockSpec((1, rows, width), lambda i: (0, i, 0)),
        ]
        + [spec] * len(parts)
        + [ANY] * len(tokens),
        out_specs=spec,
        out_shape=jax.ShapeDtypeStruct((local, width), BF),
        compiler_params=params(16),
        cost_estimate=SMALL,
    )(checkpoint, gain, kept, *parts, *tokens)


def blocks_kernel(order_ref, weight_ref, *refs):
    out_ref, held, done = refs[-3:]
    columns = weight_ref.shape[-1]
    fine = weight_ref.shape[2]
    count = T // 2
    copies = [
        pltpu.make_async_copy(refs[3 * half].at[0], held.at[half], done.at[half]) for half in range(2)
    ]
    for copy in copies:
        copy.start()
    for copy in copies:
        copy.wait()
    dots = [jnp.zeros((fine, 1), F32) for _ in range(H)]
    for i in range(T):
        half = i // count
        terms = (held.at[half],) + tuple(refs[3 * half + 1 : 3 * half + 3])
        t = order_ref[i]
        for h in range(H):
            value = add(*[term[h, i % count] for term in terms]).astype(BF)
            out_ref[h * T + t, :, :columns] = value
            product = value.astype(F32) * weight_ref[t, h].astype(F32)
            dots[h] += jnp.sum(product, axis=1, keepdims=True)
    lane = lax.broadcasted_iota(jnp.int32, (fine, 128), 1)
    for h in range(H):
        high = dots[h].astype(BF).astype(F32)
        extra = jnp.where(lane == 0, high, jnp.where(lane == 1, dots[h] - high, 0.0)).astype(BF)
        for t in range(T):
            out_ref[h * T + t, :, columns:] = extra


def last_blocks(order, weight, terms, *tokens):
    fine, columns = weight.shape[2:]
    return pl.pallas_call(
        blocks_kernel,
        in_specs=[SMEM, VMEM] + [ANY, VMEM, VMEM] * 2 + [ANY] * len(tokens),
        out_specs=VMEM,
        out_shape=jax.ShapeDtypeStruct((H * T, fine, columns + 128), BF),
        scratch_shapes=[
            pltpu.VMEM((2,) + terms[1].shape, BF),
            pltpu.SemaphoreType.DMA((2,)),
        ],
        compiler_params=params(12),
        cost_estimate=SMALL,
    )(order, weight, *terms, *tokens)


def finish_kernel(group_ref, gain_ref, blocks_ref, weight_ref, gain_out_ref):
    columns = weight_ref.shape[1]
    fine = blocks_ref.shape[1]
    lane = lax.broadcasted_iota(jnp.int32, (8, 128), 1)
    pick = jnp.where(lane < 2, 1.0, 0.0).astype(BF)
    dots = jnp.zeros((8, weight_ref.shape[0]), F32)
    for h in range(H):
        extra = blocks_ref[h * T : (h + 1) * T, :, columns:].reshape(T * fine, 128)
        dots += lax.dot_general(pick, extra, (((1,), (1,)), ((), ())), preferred_element_type=F32)
    gain_out_ref[...] = dots[:1] / gain_ref[pl.ds(group_ref[0], 1), :].astype(F32)
    for t in range(T):
        weight_ref[t * fine : (t + 1) * fine] = add(
            *[blocks_ref[h * T + t, :, :columns] for h in range(H)]
        )


def finish(group, gain, blocks):
    fine, width = blocks.shape[1:]
    rows = T * fine
    weight, gain_row = pl.pallas_call(
        finish_kernel,
        in_specs=[SMEM, VMEM, VMEM],
        out_specs=[VMEM, VMEM],
        out_shape=[
            jax.ShapeDtypeStruct((rows, width - 128), F32),
            jax.ShapeDtypeStruct((1, rows), F32),
        ],
        compiler_params=params(8),
        cost_estimate=SMALL,
    )(group.reshape(1), gain.astype(F32).reshape(-1, rows), blocks)
    return weight, gain_row.reshape(rows)


def shards(checkpoint, gain, qkv_weight, qkv_cot):
    h, z, c = lax.axis_index("h"), lax.axis_index("z"), lax.axis_index("c")
    x, l = lax.axis_index("x"), lax.axis_index("l")
    local, width = checkpoint.shape
    tokens, columns = qkv_cot.shape
    grad_scale = 1.0 / math.sqrt(tokens * H * Z * C)
    fine = width // (H * Z * C * T)
    gain_row = gain.reshape(1, width)

    with jax.named_scope("normed_exchange"):
        parts = normed_parts(z, checkpoint, gain_row)
        left = lax.all_to_all(parts, ("c",) + TENSOR, 0, 0, tiled=True)
        left = left.reshape(C, tokens, Z * H * fine)

    near = {(0, 0): qkv_cot}
    with jax.named_scope("cot_gather"):
        near[0, 1] = swap(qkv_cot, "l")
        for step in (1, 3):
            near[step, 0] = shift(qkv_cot, "x", -step)
        near[2, 0] = shift(after(qkv_cot, parts), "x", -2)

    with jax.named_scope("input_terms"):
        cot_near = relative(qkv_cot.reshape(X, L, local, columns), x, l)
        kept, multiplied, sent = grad_terms(cot_near.reshape(tokens, columns), qkv_weight, parts)

    keys = (((0, 0), (0, 1), (1, 0), (3, 0)), ((2, 0), (1, 1), (3, 1), (2, 1)))
    across = {(0, 0): swap(after(qkv_cot, parts), "c")}

    def product(some, going, *given):
        own, other = [near[key] for key in some], [across[key] for key in some]
        return weight_terms(c, left, own, other, grad_scale, going, *given)

    with jax.named_scope("cot_gather"):
        for key in ((0, 1), (1, 0), (3, 0), (2, 0)):
            near[key] = after(near[key], multiplied, left)
        near[3, 1] = shift(near[0, 1], "x", 1)
        near[1, 1] = shift(near[0, 1], "x", -1)
        near[2, 1] = swap(near[2, 0], "l")
        for key in keys[0][1:]:
            across[key] = swap(near[key], "c")
    with jax.named_scope("weight_terms"):
        a, a_4, a_5 = product(keys[0], (4, 5), multiplied)
    with jax.named_scope("cot_gather"):
        for key in keys[1]:
            near[key] = after(near[key], a_4)
            across[key] = swap(near[key], "c")
    with jax.named_scope("weight_terms"):
        b, b_3, b_4 = product(keys[1], (3, 4), a_4)

    with jax.named_scope("chains"):
        up = lambda value: shift(value, "z", 1)
        down = lambda value: shift(value, "z", -1)
        sent = dict(zip(SENT, after(sent, near[1, 1], near[3, 1])))
        up_a, down_a = up(a_4), down(a_5)
        far_up, far_down = shift(sent[2, 0], "x", 1), shift(sent[2, 1], "x", -1)
        up_1 = shift(sent[1, 1], "x", 1)
        up_b, down_b = up(b_3), down(b_4)
        s1 = sums([(a, 3, up_a), (a, 6, down_a)], b_3)
        up_a, down_a = up(s1[0]), down(s1[1])
        s2 = sums([(kept, 3, far_down), (kept, 2, far_up)], s1[0])
        down_1, up_0 = shift(s2[0], "x", -1), shift(s2[1], "x", 1)
        down_0 = shift(after(sent[3, 0], s2[0]), "x", -1)
        s3 = sums([(b, 2, up_b), (b, 5, down_b)], s2[0])
        up_b, down_b = up(s3[0]), down(s3[1])
        s4 = sums([(a, 2, up_a), (a, 7, down_a)], s3[0])
        up_a, down_a = up(s4[0]), down(s4[1])
        s5 = sums([(b, 1, up_b), (b, 6, down_b)], s4[0])
        up_b, down_b = up(s5[0]), down(s5[1])
        s6 = sums([(kept, 1, up_1, down_1)], s5[0])
        other_l = swap(s6[0], "l")
        s7 = sums([(a, 1, up_a)], s6[0])
        up_a = up(s7[0])
        s8 = sums([(b, 7, down_b)], s7[0], up_0, down_0)
        down_b = down(s8[0])

    with jax.named_scope("weight_rows"):
        mine = qkv_weight.reshape(H, Z, C, T, fine, columns)
        mine = lax.dynamic_slice(mine, (0, z, c, 0, 0, 0), (H, 1, 1, T, fine, columns))
        mine = after(mine.reshape(H, T, fine, columns), s3[0])
        mine = lax.all_to_all(mine.swapaxes(0, 1), TENSOR, 0, 0, tiled=True)

    with jax.named_scope("input_out"):
        input_grad = input_out(checkpoint, gain_row, kept, (up_0, down_0, other_l), s8[0])

    with jax.named_scope("weight_out"):
        order = jnp.stack(
            [lax.rem(x + i, X) * L + lax.rem(l + j, L) for some in keys for i, j in some]
        )
        blocks = last_blocks(order, mine, (a, up_a, down_a, b, up_b, down_b), other_l)
        blocks = lax.all_to_all(blocks, ("h",) + TENSOR, 0, 0, tiled=True)
        weight_out, gain_out = finish((h * Z + z) * C + c, gain, blocks)
    return (input_grad, gain_out, weight_out)


def solution(mesh):
    fine_mesh = Mesh(mesh.devices.reshape(H, Z, C, X, L), DP + TENSOR)
    rows = P(DP + TENSOR, None)
    in_specs = (rows, P(), P(None, TENSOR), P(DP, TENSOR))
    out_specs = (rows, P(DP), P(DP, TENSOR))
    return jax.shard_map(
        shards, mesh=fine_mesh, in_specs=in_specs, out_specs=out_specs, check_vma=False
    )
```

```python
import functools
import math

import jax
import jax.numpy as jnp
from jax import lax
from jax.experimental import pallas as pl
from jax.experimental.pallas import tpu as pltpu
from jax.sharding import Mesh
from jax.sharding import PartitionSpec as P

H, Z, C, X, L = 2, 8, 2, 4, 2
T = X * L
DP = ("h", "z", "c")
TENSOR = ("x", "l")
BF = jnp.bfloat16
F32 = jnp.float32

VMEM = pl.BlockSpec(memory_space=pltpu.VMEM)
SMEM = pl.BlockSpec(memory_space=pltpu.SMEM)
ANY = pl.BlockSpec(memory_space=pl.ANY)


def params(mib):
    return pltpu.CompilerParams(vmem_limit_bytes=mib << 20)


def cost(flops, bytes_accessed):
    return pl.CostEstimate(flops=flops, bytes_accessed=bytes_accessed, transcendentals=0)


SMALL = cost(1000, 1000)


def shift(value, axis, step):
    n = lax.axis_size(axis)
    return lax.ppermute(value, axis, [(i, (i + step) % n) for i in range(n)])


def swap(value, axis):
    return shift(value, axis, 1)


def relative(blocks, x, l):
    turned = lax.dynamic_slice_in_dim(jnp.concatenate([blocks, blocks], 0), x, X, 0)
    return jnp.where(l == 0, turned, turned[:, ::-1])


def after(values, *others):
    return lax.optimization_barrier((values, *others))[0]


def add(*values):
    total = values[0].astype(F32)
    for value in values[1:]:
        total = total + value.astype(F32)
    return total


def normed_kernel(z_ref, check_ref, gain_ref, out_ref, normed_ref):
    local, width = check_ref.shape
    span = width // (H * Z * C)
    fine = span // T
    per = 128 // fine
    values = check_ref[...].astype(F32)
    inv_rms = lax.rsqrt(jnp.mean(values * values, axis=1, keepdims=True) + 1e-05)
    normed_ref[...] = (values * inv_rms * gain_ref[...].astype(F32)).astype(BF)
    groups = Z * H // per
    lines = []
    for c in range(C):
        for group in range(groups):
            pieces = []
            for piece in range(per):
                k, h = divmod(group * per + piece, H)
                at = ((h * Z + lax.rem(z_ref[0] + k, Z)) * C + c) * span
                pieces.append(normed_ref[:, pl.ds(pl.multiple_of(at, span), span)])
            lines.append(jnp.concatenate(pieces, axis=1))
    stacked = jnp.concatenate(lines, axis=0)
    size = per * span
    row = lax.broadcasted_iota(jnp.int32, (size, size), 0)
    column = lax.broadcasted_iota(jnp.int32, (size, size), 1)
    k, t, i = row // span, (row // fine) % T, row % fine
    places = jnp.where(column == t * 128 + k * fine + i, 1.0, 0.0).astype(BF)
    placed = jnp.dot(stacked, places, preferred_element_type=F32).astype(BF)
    for c in range(C):
        for group in range(groups):
            at = (c * groups + group) * local
            for t in range(T):
                out_ref[c * T + t, :, group * 128 : (group + 1) * 128] = placed[
                    at : at + local, t * 128 : (t + 1) * 128
                ]


def normed_parts(z, checkpoint, gain):
    local, width = checkpoint.shape
    return pl.pallas_call(
        normed_kernel,
        in_specs=[SMEM, VMEM, VMEM],
        out_specs=VMEM,
        out_shape=jax.ShapeDtypeStruct((C * T, local, width // (C * T)), BF),
        scratch_shapes=[pltpu.VMEM((local, width), BF)],
        compiler_params=params(20),
        cost_estimate=cost(2 * local * width * 1024, 4 * local * width),
    )(z.reshape(1), checkpoint, gain)


KEPT = ((0, 0), (0, 1), (1, 0), (3, 1))
SENT = ((2, 0), (2, 1), (1, 1), (3, 0))


def terms_kernel(cot_ref, w_ref, *refs):
    kept, token = refs[-T // 2 - 2 : -T // 2]
    sent = refs[-T // 2 :]
    token[...] = jnp.zeros(token.shape, F32)
    product = lax.dot_general(
        cot_ref[...], w_ref[...], (((1,), (1,)), ((), ())), preferred_element_type=F32
    )
    rows = product.shape[0] // T
    block = lambda dx, dl: product[(dx * L + dl) * rows :][:rows].astype(BF)
    for i, key in enumerate(KEPT):
        kept[i] = block(*key)
    for key, out in zip(SENT, sent):
        out[...] = block(*key)


def grad_terms(cot, weight, *tokens, tile=2048):
    rows, depth = cot.shape
    width = weight.shape[0]
    own = rows // T
    outs = pl.pallas_call(
        terms_kernel,
        grid=(width // tile,),
        in_specs=[
            pl.BlockSpec((rows, depth), lambda i: (0, 0)),
            pl.BlockSpec((tile, depth), lambda i: (i, 0)),
        ]
        + [ANY] * len(tokens),
        out_specs=[
            pl.BlockSpec((len(KEPT), own, tile), lambda i: (0, 0, i)),
            pl.BlockSpec((8, 128), lambda i: (0, 0)),
        ]
        + [pl.BlockSpec((own, tile), lambda i: (0, i))] * len(SENT),
        out_shape=[
            jax.ShapeDtypeStruct((len(KEPT), own, width), BF),
            jax.ShapeDtypeStruct((8, 128), F32),
        ]
        + [jax.ShapeDtypeStruct((own, width), BF)] * len(SENT),
        compiler_params=params(58),
        cost_estimate=cost(
            4 * rows * depth * width, 2 * (rows * depth + width * depth + rows * width)
        ),
    )(cot, weight, *tokens)
    return outs[0], outs[1], outs[2:]


def weight_kernel(scale, count, sent, core_ref, left_ref, *refs):
    kept, turned = refs[-len(sent) - 2], refs[-1]
    outs = refs[-len(sent) - 1 : -1]
    tokens = left_ref.shape[1]

    @pl.when(pl.program_id(0) == 0)
    def _():
        turned[:, :tokens] = left_ref[core_ref[0]].T
        turned[:, tokens:] = left_ref[1 - core_ref[0]].T

    for i in range(count):

        @pl.when(pl.program_id(0) == i)
        def _():
            right = jnp.concatenate([refs[i][...], refs[count + i][...]], axis=0)
            product = jnp.dot(turned[...], right, preferred_element_type=F32)
            product = (product * scale).astype(BF)
            kept[...] = product.reshape(kept.shape)
            rows = product.shape[0] // Z
            for k, out in zip(sent, outs):
                out[...] = product[k * rows : (k + 1) * rows].reshape(out.shape)


def weight_terms(core, left, own, other, scale, sent, *tokens):
    cores, rows, features = left.shape
    columns = own[0].shape[1]
    count = len(own)
    fine = features // (Z * H)
    whole = lambda shape: pl.BlockSpec(shape, lambda i: (0,) * len(shape))
    return pl.pallas_call(
        functools.partial(weight_kernel, scale, count, sent),
        grid=(count,),
        in_specs=[SMEM, whole(left.shape)]
        + [whole(own[0].shape)] * (2 * count)
        + [ANY] * len(tokens),
        out_specs=[pl.BlockSpec((Z, H, 1, fine, columns), lambda i: (0, 0, i, 0, 0))]
        + [pl.BlockSpec((H, 1, fine, columns), lambda i: (0, i, 0, 0))] * len(sent),
        out_shape=[jax.ShapeDtypeStruct((Z, H, count, fine, columns), BF)]
        + [jax.ShapeDtypeStruct((H, count, fine, columns), BF)] * len(sent),
        scratch_shapes=[pltpu.VMEM((features, cores * rows), BF)],
        compiler_params=params(58),
        cost_estimate=SMALL,
    )(core.reshape(1), left, *own, *other, *tokens)


def sums_kernel(groups, *refs):
    count = len(groups)
    outs, held, done = (refs[len(refs) - i * count :][:count] for i in (3, 2, 1))
    at, copies, others = 0, [], []
    for (index, size), buffer, semaphore in zip(groups, held, done):
        copies.append(pltpu.make_async_copy(refs[at].at[index], buffer, semaphore))
        copies[-1].start()
        others.append(refs[at + 1 : at + size])
        at += size
    for copy, buffer, other, out in zip(copies, held, others, outs):
        copy.wait()
        out[...] = add(buffer[...], *[ref[...] for ref in other]).astype(BF)


def sums(groups, *tokens):
    shape = groups[0][2].shape
    specs, values = [], []
    for stack, _, *arrays in groups:
        specs += [ANY] + [VMEM] * len(arrays)
        values += [stack] + arrays
    return pl.pallas_call(
        functools.partial(sums_kernel, [(group[1], len(group) - 1) for group in groups]),
        in_specs=specs + [ANY] * len(tokens),
        out_specs=[VMEM] * len(groups),
        out_shape=[jax.ShapeDtypeStruct(shape, BF) for group in groups],
        scratch_shapes=[pltpu.VMEM(shape, BF)] * len(groups)
        + [pltpu.SemaphoreType.DMA(())] * len(groups),
        compiler_params=params(12),
        cost_estimate=SMALL,
    )(*values, *tokens)


def input_kernel(check_ref, gain_ref, kept_ref, *refs):
    out_ref = refs[-1]
    values = check_ref[...].astype(F32)
    inv_rms = lax.rsqrt(jnp.mean(values * values, axis=1, keepdims=True) + 1e-05)
    unit_rows = values * inv_rms
    scaled = add(kept_ref[0], *[ref[...] for ref in refs[:3]]) * gain_ref[...].astype(F32)
    mean = jnp.mean(scaled * unit_rows, axis=1, keepdims=True)
    out_ref[...] = (inv_rms * (scaled - unit_rows * mean)).astype(BF)


def input_out(checkpoint, gain, kept, parts, *tokens, rows=16):
    local, width = checkpoint.shape
    spec = pl.BlockSpec((rows, width), lambda i: (i, 0))
    return pl.pallas_call(
        input_kernel,
        grid=(local // rows,),
        in_specs=[
            spec,
            pl.BlockSpec((1, width), lambda i: (0, 0)),
            pl.BlockSpec((1, rows, width), lambda i: (0, i, 0)),
        ]
        + [spec] * len(parts)
        + [ANY] * len(tokens),
        out_specs=spec,
        out_shape=jax.ShapeDtypeStruct((local, width), BF),
        compiler_params=params(16),
        cost_estimate=SMALL,
    )(checkpoint, gain, kept, *parts, *tokens)


def blocks_kernel(order_ref, weight_ref, *refs):
    out_ref, held, done = refs[-3:]
    columns = weight_ref.shape[-1]
    fine = weight_ref.shape[2]
    count = T // 2
    copies = [
        pltpu.make_async_copy(refs[3 * half].at[0], held.at[half], done.at[half]) for half in range(2)
    ]
    for copy in copies:
        copy.start()
    for copy in copies:
        copy.wait()
    dots = [jnp.zeros((fine, 1), F32) for _ in range(H)]
    for i in range(T):
        half = i // count
        terms = (held.at[half],) + tuple(refs[3 * half + 1 : 3 * half + 3])
        t = order_ref[i]
        for h in range(H):
            value = add(*[term[h, i % count] for term in terms]).astype(BF)
            out_ref[h * T + t, :, :columns] = value
            product = value.astype(F32) * weight_ref[t, h].astype(F32)
            dots[h] += jnp.sum(product, axis=1, keepdims=True)
    lane = lax.broadcasted_iota(jnp.int32, (fine, 128), 1)
    for h in range(H):
        high = dots[h].astype(BF).astype(F32)
        extra = jnp.where(lane == 0, high, jnp.where(lane == 1, dots[h] - high, 0.0)).astype(BF)
        for t in range(T):
            out_ref[h * T + t, :, columns:] = extra


def last_blocks(order, weight, terms, *tokens):
    fine, columns = weight.shape[2:]
    return pl.pallas_call(
        blocks_kernel,
        in_specs=[SMEM, VMEM] + [ANY, VMEM, VMEM] * 2 + [ANY] * len(tokens),
        out_specs=VMEM,
        out_shape=jax.ShapeDtypeStruct((H * T, fine, columns + 128), BF),
        scratch_shapes=[
            pltpu.VMEM((2,) + terms[1].shape, BF),
            pltpu.SemaphoreType.DMA((2,)),
        ],
        compiler_params=params(12),
        cost_estimate=SMALL,
    )(order, weight, *terms, *tokens)


def finish_kernel(group_ref, gain_ref, blocks_ref, *refs):
    weight_ref, gain_out_ref = refs[-2:]
    columns = weight_ref.shape[1]
    fine = blocks_ref.shape[1]
    lane = lax.broadcasted_iota(jnp.int32, (8, 128), 1)
    pick = jnp.where(lane < 2, 1.0, 0.0).astype(BF)
    dots = jnp.zeros((8, weight_ref.shape[0]), F32)
    for h in range(H):
        extra = blocks_ref[h * T : (h + 1) * T, :, columns:].reshape(T * fine, 128)
        dots += lax.dot_general(pick, extra, (((1,), (1,)), ((), ())), preferred_element_type=F32)
    gain_out_ref[...] = dots[:1] / gain_ref[pl.ds(group_ref[0], 1), :].astype(F32)
    for t in range(T):
        weight_ref[t * fine : (t + 1) * fine] = add(
            *[blocks_ref[h * T + t, :, :columns] for h in range(H)]
        )


def finish(group, gain, blocks, *tokens):
    fine, width = blocks.shape[1:]
    rows = T * fine
    weight, gain_row = pl.pallas_call(
        finish_kernel,
        in_specs=[SMEM, VMEM, VMEM] + [ANY] * len(tokens),
        out_specs=[VMEM, VMEM],
        out_shape=[
            jax.ShapeDtypeStruct((rows, width - 128), F32),
            jax.ShapeDtypeStruct((1, rows), F32),
        ],
        compiler_params=params(8),
        cost_estimate=SMALL,
    )(group.reshape(1), gain.astype(F32).reshape(-1, rows), blocks, *tokens)
    return weight, gain_row.reshape(rows)


def shards(checkpoint, gain, qkv_weight, qkv_cot):
    h, z, c = lax.axis_index("h"), lax.axis_index("z"), lax.axis_index("c")
    x, l = lax.axis_index("x"), lax.axis_index("l")
    local, width = checkpoint.shape
    tokens, columns = qkv_cot.shape
    grad_scale = 1.0 / math.sqrt(tokens * H * Z * C)
    fine = width // (H * Z * C * T)
    gain_row = gain.reshape(1, width)

    with jax.named_scope("normed_exchange"):
        parts = normed_parts(z, checkpoint, gain_row)
        left = lax.all_to_all(parts, ("c",) + TENSOR, 0, 0, tiled=True)
        left = left.reshape(C, tokens, Z * H * fine)

    near = {(0, 0): qkv_cot}
    with jax.named_scope("cot_gather"):
        near[0, 1] = swap(qkv_cot, "l")
        for step in (1, 3):
            near[step, 0] = shift(qkv_cot, "x", -step)

    with jax.named_scope("input_terms"):
        cot_near = relative(qkv_cot.reshape(X, L, local, columns), x, l)
        kept, multiplied, sent = grad_terms(cot_near.reshape(tokens, columns), qkv_weight, parts)

    keys = (((0, 0), (0, 1), (1, 0), (3, 0)), ((2, 0), (1, 1), (3, 1), (2, 1)))
    across = {(0, 0): swap(after(qkv_cot, parts), "c")}

    def product(some, going, *given):
        own, other = [near[key] for key in some], [across[key] for key in some]
        return weight_terms(c, left, own, other, grad_scale, going, *given)

    with jax.named_scope("cot_gather"):
        near[2, 0] = shift(after(qkv_cot, multiplied), "x", -2)
        for key in ((0, 1), (1, 0), (3, 0)):
            near[key] = after(near[key], multiplied, left)
        near[3, 1] = shift(near[0, 1], "x", 1)
        near[1, 1] = shift(near[0, 1], "x", -1)
        for key in keys[0][1:]:
            across[key] = swap(near[key], "c")
    with jax.named_scope("weight_terms"):
        a, a_4, a_5 = product(keys[0], (4, 5), multiplied)
    with jax.named_scope("cot_gather"):
        near[2, 0] = after(near[2, 0], a_4)
        near[2, 1] = swap(near[2, 0], "l")
        for key in keys[1]:
            if key[0] != 2:
                near[key] = after(near[key], a_4)
            across[key] = swap(near[key], "c")
    with jax.named_scope("weight_terms"):
        b, b_3, b_4 = product(keys[1], (3, 4), a_4)

    with jax.named_scope("chains"):
        up = lambda value: shift(value, "z", 1)
        down = lambda value: shift(value, "z", -1)
        up_a, down_a = up(a_4), down(a_5)
        up_b, down_b = up(b_3), down(b_4)
        s1 = sums([(a, 3, up_a), (a, 6, down_a)], b_3)
        up_a, down_a = up(s1[0]), down(s1[1])
        sent = dict(zip(SENT, after(sent, s1[0])))
        far_up, far_down = shift(sent[2, 0], "x", 1), shift(sent[2, 1], "x", -1)
        s3 = sums([(b, 2, up_b), (b, 5, down_b)], s1[0])
        up_b, down_b = up(s3[0]), down(s3[1])
        s4 = sums([(a, 2, up_a), (a, 7, down_a)], s3[0])
        up_a, down_a = up(s4[0]), down(s4[1])
        s2 = sums([(kept, 3, far_down), (kept, 2, far_up)], s4[0])
        down_1, up_1 = shift(s2[0], "x", -1), shift(after(sent[1, 1], s2[0]), "x", 1)
        s5 = sums([(b, 1, up_b), (b, 6, down_b)], s2[0])
        up_b, down_b = up(s5[0]), down(s5[1])
        s7 = sums([(a, 1, up_a)], s5[0])
        up_a = up(s7[0])
        up_0, down_0 = shift(after(s2[1], s7[0]), "x", 1), shift(after(sent[3, 0], s7[0]), "x", -1)
        s8 = sums([(b, 7, down_b)], s7[0])
        down_b = down(s8[0])
        s6 = sums([(kept, 1, up_1, down_1)], s8[0])
        other_l = swap(s6[0], "l")

    with jax.named_scope("weight_rows"):
        mine = qkv_weight.reshape(H, Z, C, T, fine, columns)
        mine = lax.dynamic_slice(mine, (0, z, c, 0, 0, 0), (H, 1, 1, T, fine, columns))
        mine = after(mine.reshape(H, T, fine, columns), s3[0])
        mine = lax.all_to_all(mine.swapaxes(0, 1), TENSOR, 0, 0, tiled=True)

    with jax.named_scope("input_out"):
        input_grad = input_out(checkpoint, gain_row, kept, (up_0, down_0, other_l), s8[0])

    with jax.named_scope("weight_out"):
        order = jnp.stack(
            [lax.rem(x + i, X) * L + lax.rem(l + j, L) for some in keys for i, j in some]
        )
        blocks = last_blocks(order, mine, (a, up_a, down_a, b, up_b, down_b), s6[0])
        blocks = lax.all_to_all(blocks, ("h",) + TENSOR, 0, 0, tiled=True)
        weight_out, gain_out = finish((h * Z + z) * C + c, gain, blocks, input_grad)
    return (input_grad, gain_out, weight_out)


def solution(mesh):
    fine_mesh = Mesh(mesh.devices.reshape(H, Z, C, X, L), DP + TENSOR)
    rows = P(DP + TENSOR, None)
    in_specs = (rows, P(), P(None, TENSOR), P(DP, TENSOR))
    out_specs = (rows, P(DP), P(DP, TENSOR))
    return jax.shard_map(
        shards, mesh=fine_mesh, in_specs=in_specs, out_specs=out_specs, check_vma=False
    )
```

```python
import functools
import math

import jax
import jax.numpy as jnp
from jax import lax
from jax.experimental import pallas as pl
from jax.experimental.pallas import tpu as pltpu
from jax.sharding import Mesh
from jax.sharding import PartitionSpec as P

H, Z, C, X, L = 2, 8, 2, 4, 2
T = X * L
DP = ("h", "z", "c")
TENSOR = ("x", "l")
BF = jnp.bfloat16
F32 = jnp.float32

VMEM = pl.BlockSpec(memory_space=pltpu.VMEM)
SMEM = pl.BlockSpec(memory_space=pltpu.SMEM)
ANY = pl.BlockSpec(memory_space=pl.ANY)


def params(mib):
    return pltpu.CompilerParams(vmem_limit_bytes=mib << 20)


def cost(flops, bytes_accessed):
    return pl.CostEstimate(flops=flops, bytes_accessed=bytes_accessed, transcendentals=0)


def shift(value, axis, step):
    n = lax.axis_size(axis)
    return lax.ppermute(value, axis, [(i, (i + step) % n) for i in range(n)])


def swap(value, axis):
    return shift(value, axis, 1)


def relative(blocks, x, l):
    turned = lax.dynamic_slice_in_dim(jnp.concatenate([blocks, blocks], 0), x, X, 0)
    return jnp.where(l == 0, turned, turned[:, ::-1])


def after(values, *others):
    return lax.optimization_barrier((values, *others))[0]


def add(*values):
    total = values[0].astype(F32)
    for value in values[1:]:
        total = total + value.astype(F32)
    return total


def normed_kernel(z_ref, check_ref, gain_ref, out_ref, normed_ref):
    local, width = check_ref.shape
    span = width // (H * Z * C)
    fine = span // T
    per = 128 // fine
    values = check_ref[...].astype(F32)
    inv_rms = lax.rsqrt(jnp.mean(values * values, axis=1, keepdims=True) + 1e-05)
    normed_ref[...] = (values * inv_rms * gain_ref[...].astype(F32)).astype(BF)
    groups = Z * H // per
    lines = []
    for c in range(C):
        for group in range(groups):
            pieces = []
            for piece in range(per):
                k, h = divmod(group * per + piece, H)
                at = ((h * Z + lax.rem(z_ref[0] + k, Z)) * C + c) * span
                pieces.append(normed_ref[:, pl.ds(pl.multiple_of(at, span), span)])
            lines.append(jnp.concatenate(pieces, axis=1))
    stacked = jnp.concatenate(lines, axis=0)
    size = per * span
    row = lax.broadcasted_iota(jnp.int32, (size, size), 0)
    column = lax.broadcasted_iota(jnp.int32, (size, size), 1)
    k, t, i = row // span, (row // fine) % T, row % fine
    places = jnp.where(column == t * 128 + k * fine + i, 1.0, 0.0).astype(BF)
    placed = jnp.dot(stacked, places, preferred_element_type=F32).astype(BF)
    for c in range(C):
        for group in range(groups):
            at = (c * groups + group) * local
            for t in range(T):
                out_ref[c * T + t, :, group * 128 : (group + 1) * 128] = placed[
                    at : at + local, t * 128 : (t + 1) * 128
                ]


def normed_parts(z, checkpoint, gain):
    local, width = checkpoint.shape
    return pl.pallas_call(
        normed_kernel,
        in_specs=[SMEM, VMEM, VMEM],
        out_specs=VMEM,
        out_shape=jax.ShapeDtypeStruct((C * T, local, width // (C * T)), BF),
        scratch_shapes=[pltpu.VMEM((local, width), BF)],
        compiler_params=params(20),
        cost_estimate=cost(2 * local * width * 1024, 4 * local * width),
    )(z.reshape(1), checkpoint, gain)


def terms_kernel(cot_ref, w_ref, *refs):
    outs, token = refs[-T - 1 : -1], refs[-1]
    token[...] = jnp.zeros(token.shape, F32)
    product = lax.dot_general(
        cot_ref[...], w_ref[...], (((1,), (1,)), ((), ())), preferred_element_type=F32
    )
    rows = product.shape[0] // T
    for i, out in enumerate(outs):
        out[...] = product[i * rows : (i + 1) * rows].astype(BF)


def grad_terms(cot, weight, *tokens, tile=2048):
    rows, depth = cot.shape
    width = weight.shape[0]
    own = rows // T
    outs = pl.pallas_call(
        terms_kernel,
        grid=(width // tile,),
        in_specs=[
            pl.BlockSpec((rows, depth), lambda i: (0, 0)),
            pl.BlockSpec((tile, depth), lambda i: (i, 0)),
        ]
        + [ANY] * len(tokens),
        out_specs=[pl.BlockSpec((own, tile), lambda i: (0, i))] * T
        + [pl.BlockSpec((8, 128), lambda i: (0, 0))],
        out_shape=[jax.ShapeDtypeStruct((own, width), BF)] * T
        + [jax.ShapeDtypeStruct((8, 128), F32)],
        compiler_params=params(58),
        cost_estimate=cost(
            4 * rows * depth * width, 2 * (rows * depth + width * depth + rows * width)
        ),
    )(cot, weight, *tokens)
    return outs[:T], outs[T]


def weight_kernel(scale, count, core_ref, left_ref, *refs):
    outs = refs[-Z - 1 : -1]
    turned = refs[-1]
    tokens = left_ref.shape[1]

    @pl.when(pl.program_id(0) == 0)
    def _():
        turned[:, :tokens] = left_ref[core_ref[0]].T
        turned[:, tokens:] = left_ref[1 - core_ref[0]].T

    for i in range(count):

        @pl.when(pl.program_id(0) == i)
        def _():
            right = jnp.concatenate([refs[i][...], refs[count + i][...]], axis=0)
            product = jnp.dot(turned[...], right, preferred_element_type=F32)
            product = (product * scale).astype(BF)
            rows = product.shape[0] // Z
            for k, out in enumerate(outs):
                out[...] = product[k * rows : (k + 1) * rows].reshape(out.shape)


def weight_terms(core, left, own, other, scale, *tokens):
    cores, rows, features = left.shape
    columns = own[0].shape[1]
    count = len(own)
    fine = features // (Z * H)
    whole = lambda shape: pl.BlockSpec(shape, lambda i: (0,) * len(shape))
    return pl.pallas_call(
        functools.partial(weight_kernel, scale, count),
        grid=(count,),
        in_specs=[SMEM, whole(left.shape)]
        + [whole(own[0].shape)] * (2 * count)
        + [ANY] * len(tokens),
        out_specs=[pl.BlockSpec((H, 1, fine, columns), lambda i: (0, i, 0, 0))] * Z,
        out_shape=[jax.ShapeDtypeStruct((H, count, fine, columns), BF)] * Z,
        scratch_shapes=[pltpu.VMEM((features, cores * rows), BF)],
        compiler_params=params(58),
        cost_estimate=cost(
            2 * features * cores * rows * columns * count,
            2 * (features * cores * rows + (cores * rows + features) * columns * count),
        ),
    )(core.reshape(1), left, *own, *other, *tokens)


def sums_kernel(sizes, *refs):
    outs = refs[-len(sizes) :]
    at = 0
    for size, out in zip(sizes, outs):
        out[...] = add(*[ref[...] for ref in refs[at : at + size]]).astype(BF)
        at += size


def sums(groups, *tokens, steps=1):
    values = [value for group in groups for value in group]
    shape = values[0].shape
    block = shape[:-1] + (shape[-1] // steps,)
    spec = pl.BlockSpec(block, lambda i: (0,) * (len(shape) - 1) + (i,))
    return pl.pallas_call(
        functools.partial(sums_kernel, [len(group) for group in groups]),
        grid=(steps,),
        in_specs=[spec] * len(values) + [ANY] * len(tokens),
        out_specs=[spec] * len(groups),
        out_shape=[jax.ShapeDtypeStruct(shape, BF) for group in groups],
        compiler_params=params(16),
        cost_estimate=cost(values[0].size * len(values), 2 * values[0].size * len(values)),
    )(*values, *tokens)


def input_kernel(check_ref, gain_ref, *refs):
    out_ref = refs[-1]
    values = check_ref[...].astype(F32)
    inv_rms = lax.rsqrt(jnp.mean(values * values, axis=1, keepdims=True) + 1e-05)
    unit_rows = values * inv_rms
    scaled = add(*[ref[...] for ref in refs[:4]]) * gain_ref[...].astype(F32)
    mean = jnp.mean(scaled * unit_rows, axis=1, keepdims=True)
    out_ref[...] = (inv_rms * (scaled - unit_rows * mean)).astype(BF)


def input_out(checkpoint, gain, parts, *tokens, rows=16):
    local, width = checkpoint.shape
    spec = pl.BlockSpec((rows, width), lambda i: (i, 0))
    return pl.pallas_call(
        input_kernel,
        grid=(local // rows,),
        in_specs=[spec, pl.BlockSpec((1, width), lambda i: (0, 0))]
        + [spec] * len(parts)
        + [ANY] * len(tokens),
        out_specs=spec,
        out_shape=jax.ShapeDtypeStruct((local, width), BF),
        compiler_params=params(24),
        cost_estimate=cost(12 * local * width, 12 * local * width),
    )(checkpoint, gain, *parts, *tokens)


def blocks_kernel(order_ref, weight_ref, *refs):
    out_ref = refs[-1]
    columns = weight_ref.shape[-1]
    fine = weight_ref.shape[2]
    count = T // 2
    dots = [jnp.zeros((fine, 1), F32) for _ in range(H)]
    for i in range(T):
        terms = refs[3 * (i // count) : 3 * (i // count) + 3]
        t = order_ref[i]
        for h in range(H):
            value = add(*[term[h, i % count] for term in terms]).astype(BF)
            out_ref[h * T + t, :, :columns] = value
            product = value.astype(F32) * weight_ref[t, h].astype(F32)
            dots[h] += jnp.sum(product, axis=1, keepdims=True)
    lane = lax.broadcasted_iota(jnp.int32, (fine, 128), 1)
    for h in range(H):
        high = dots[h].astype(BF).astype(F32)
        extra = jnp.where(lane == 0, high, jnp.where(lane == 1, dots[h] - high, 0.0)).astype(BF)
        for t in range(T):
            out_ref[h * T + t, :, columns:] = extra


def last_blocks(order, weight, terms, *tokens):
    fine, columns = weight.shape[2:]
    return pl.pallas_call(
        blocks_kernel,
        in_specs=[SMEM] + [VMEM] * (1 + len(terms)) + [ANY] * len(tokens),
        out_specs=VMEM,
        out_shape=jax.ShapeDtypeStruct((H * T, fine, columns + 128), BF),
        compiler_params=params(8),
        cost_estimate=cost(5 << 20, 5 << 20),
    )(order, weight, *terms, *tokens)


def finish_kernel(group_ref, gain_ref, blocks_ref, weight_ref, gain_out_ref):
    columns = weight_ref.shape[1]
    fine = blocks_ref.shape[1]
    lane = lax.broadcasted_iota(jnp.int32, (8, 128), 1)
    pick = jnp.where(lane < 2, 1.0, 0.0).astype(BF)
    dots = jnp.zeros((8, weight_ref.shape[0]), F32)
    for h in range(H):
        extra = blocks_ref[h * T : (h + 1) * T, :, columns:].reshape(T * fine, 128)
        dots += lax.dot_general(pick, extra, (((1,), (1,)), ((), ())), preferred_element_type=F32)
    gain_out_ref[...] = dots[:1] / gain_ref[pl.ds(group_ref[0], 1), :].astype(F32)
    for t in range(T):
        weight_ref[t * fine : (t + 1) * fine] = add(
            *[blocks_ref[h * T + t, :, :columns] for h in range(H)]
        )


def finish(group, gain, blocks):
    fine, width = blocks.shape[1:]
    rows = T * fine
    weight, gain_row = pl.pallas_call(
        finish_kernel,
        in_specs=[SMEM, VMEM, VMEM],
        out_specs=[VMEM, VMEM],
        out_shape=[
            jax.ShapeDtypeStruct((rows, width - 128), F32),
            jax.ShapeDtypeStruct((1, rows), F32),
        ],
        compiler_params=params(8),
        cost_estimate=cost(5 << 20, 5 << 20),
    )(group.reshape(1), gain.astype(F32).reshape(-1, rows), blocks)
    return weight, gain_row.reshape(rows)


def shards(checkpoint, gain, qkv_weight, qkv_cot):
    h, z, c = lax.axis_index("h"), lax.axis_index("z"), lax.axis_index("c")
    x, l = lax.axis_index("x"), lax.axis_index("l")
    local, width = checkpoint.shape
    tokens, columns = qkv_cot.shape
    grad_scale = 1.0 / math.sqrt(tokens * H * Z * C)
    fine = width // (H * Z * C * T)
    gain_row = gain.reshape(1, width)

    with jax.named_scope("normed_exchange"):
        parts = normed_parts(z, checkpoint, gain_row)
        left = lax.all_to_all(parts, ("c",) + TENSOR, 0, 0, tiled=True)
        left = left.reshape(C, tokens, Z * H * fine)

    near = {(0, 0): qkv_cot}
    with jax.named_scope("cot_gather"):
        near[0, 1] = swap(qkv_cot, "l")
        for step in (1, 3):
            near[step, 0] = shift(qkv_cot, "x", -step)

    with jax.named_scope("input_terms"):
        cot_near = relative(qkv_cot.reshape(X, L, local, columns), x, l)
        term, multiplied = grad_terms(cot_near.reshape(tokens, columns), qkv_weight, parts)

    keys = (((0, 0), (0, 1), (1, 0), (3, 0)), ((2, 0), (1, 1), (3, 1), (2, 1)))
    across = {(0, 0): swap(after(qkv_cot, parts), "c")}

    def product(some, *given):
        own, other = [near[key] for key in some], [across[key] for key in some]
        return weight_terms(c, left, own, other, grad_scale, *given)

    with jax.named_scope("cot_gather"):
        near[2, 0] = shift(after(qkv_cot, multiplied), "x", -2)
        for key in ((0, 1), (1, 0), (3, 0)):
            near[key] = after(near[key], multiplied, left)
        near[3, 1] = shift(near[0, 1], "x", 1)
        near[1, 1] = shift(near[0, 1], "x", -1)
        near[2, 1] = shift(near[0, 1], "x", -2)
        for key in keys[0][1:]:
            across[key] = swap(near[key], "c")
    with jax.named_scope("weight_terms"):
        a = product(keys[0], multiplied)
    with jax.named_scope("cot_gather"):
        for key in keys[1]:
            near[key] = after(near[key], a[0])
            across[key] = swap(near[key], "c")
    with jax.named_scope("weight_terms"):
        b = product(keys[1], a[0])

    with jax.named_scope("chains"):
        up = lambda value: shift(value, "z", 1)
        down = lambda value: shift(value, "z", -1)
        term = after(term, near[1, 1], near[3, 1])
        term = {(i // L, i % L): term[i] for i in range(T)}
        up_a, down_a = up(a[4]), down(a[5])
        far_up, far_down = shift(term[2, 0], "x", 1), shift(term[2, 1], "x", -1)
        up_1 = shift(term[1, 1], "x", 1)
        up_b, down_b = up(b[3]), down(b[4])
        s1 = sums([(a[3], up_a), (a[6], down_a)], b[0])
        up_a, down_a = up(s1[0]), down(s1[1])
        s2 = sums([(term[3, 1], far_down), (term[1, 0], far_up)], s1[0], steps=4)
        down_1, up_0 = shift(s2[0], "x", -1), shift(s2[1], "x", 1)
        down_0 = shift(after(term[3, 0], s2[0]), "x", -1)
        s3 = sums([(b[2], up_b), (b[5], down_b)], s2[0])
        up_b, down_b = up(s3[0]), down(s3[1])
        s4 = sums([(a[2], up_a), (a[7], down_a)], s3[0])
        up_a, down_a = up(s4[0]), down(s4[1])
        s5 = sums([(b[1], up_b), (b[6], down_b)], s4[0])
        up_b, down_b = up(s5[0]), down(s5[1])
        s6 = sums([(term[0, 1], up_1, down_1)], s5[0], steps=4)
        other_l = swap(s6[0], "l")
        s7 = sums([(a[1], up_a)], s6[0])
        up_a = up(s7[0])
        s8 = sums([(b[7], down_b)], s7[0])
        down_b = down(s8[0])

    with jax.named_scope("weight_rows"):
        mine = qkv_weight.reshape(H, Z, C, T, fine, columns)
        mine = lax.dynamic_slice(mine, (0, z, c, 0, 0, 0), (H, 1, 1, T, fine, columns))
        mine = after(mine.reshape(H, T, fine, columns), s3[0])
        mine = lax.all_to_all(mine.swapaxes(0, 1), TENSOR, 0, 0, tiled=True)

    with jax.named_scope("input_out"):
        input_grad = input_out(checkpoint, gain_row, (term[0, 0], up_0, down_0, other_l), s8[0])

    with jax.named_scope("weight_out"):
        order = jnp.stack(
            [lax.rem(x + i, X) * L + lax.rem(l + j, L) for some in keys for i, j in some]
        )
        blocks = last_blocks(order, mine, (a[0], up_a, down_a, b[0], up_b, down_b))
        blocks = lax.all_to_all(blocks, ("h",) + TENSOR, 0, 0, tiled=True)
        weight_out, gain_out = finish((h * Z + z) * C + c, gain, blocks)
    return (input_grad, gain_out, weight_out)


def solution(mesh):
    fine_mesh = Mesh(mesh.devices.reshape(H, Z, C, X, L), DP + TENSOR)
    rows = P(DP + TENSOR, None)
    in_specs = (rows, P(), P(None, TENSOR), P(DP, TENSOR))
    out_specs = (rows, P(DP), P(DP, TENSOR))
    return jax.shard_map(
        shards, mesh=fine_mesh, in_specs=in_specs, out_specs=out_specs, check_vma=False
    )
```

```python
import functools
import math

import jax
import jax.numpy as jnp
from jax import lax
from jax.experimental import pallas as pl
from jax.experimental.pallas import tpu as pltpu
from jax.sharding import Mesh
from jax.sharding import PartitionSpec as P

H, Z, C, X, L = 2, 8, 2, 4, 2
T = X * L
DP = ("h", "z", "c")
TENSOR = ("x", "l")
BF = jnp.bfloat16
F32 = jnp.float32

VMEM = pl.BlockSpec(memory_space=pltpu.VMEM)
SMEM = pl.BlockSpec(memory_space=pltpu.SMEM)
ANY = pl.BlockSpec(memory_space=pl.ANY)


def params(mib):
    return pltpu.CompilerParams(vmem_limit_bytes=mib << 20)


def cost(flops, bytes_accessed):
    return pl.CostEstimate(flops=flops, bytes_accessed=bytes_accessed, transcendentals=0)


def shift(value, axis, step):
    n = lax.axis_size(axis)
    return lax.ppermute(value, axis, [(i, (i + step) % n) for i in range(n)])


def swap(value, axis):
    return shift(value, axis, 1)


def relative(blocks, x, l):
    turned = lax.dynamic_slice_in_dim(jnp.concatenate([blocks, blocks], 0), x, X, 0)
    return jnp.where(l == 0, turned, turned[:, ::-1])


def after(values, *others):
    return lax.optimization_barrier((values, *others))[0]


def add(*values):
    total = values[0].astype(F32)
    for value in values[1:]:
        total = total + value.astype(F32)
    return total


def normed_kernel(z_ref, check_ref, gain_ref, out_ref, normed_ref):
    local, width = check_ref.shape
    span = width // (H * Z * C)
    fine = span // T
    per = 128 // fine
    values = check_ref[...].astype(F32)
    inv_rms = lax.rsqrt(jnp.mean(values * values, axis=1, keepdims=True) + 1e-05)
    normed_ref[...] = (values * inv_rms * gain_ref[...].astype(F32)).astype(BF)
    groups = Z * H // per
    lines = []
    for c in range(C):
        for group in range(groups):
            pieces = []
            for piece in range(per):
                k, h = divmod(group * per + piece, H)
                at = ((h * Z + lax.rem(z_ref[0] + k, Z)) * C + c) * span
                pieces.append(normed_ref[:, pl.ds(pl.multiple_of(at, span), span)])
            lines.append(jnp.concatenate(pieces, axis=1))
    stacked = jnp.concatenate(lines, axis=0)
    size = per * span
    row = lax.broadcasted_iota(jnp.int32, (size, size), 0)
    column = lax.broadcasted_iota(jnp.int32, (size, size), 1)
    k, t, i = row // span, (row // fine) % T, row % fine
    places = jnp.where(column == t * 128 + k * fine + i, 1.0, 0.0).astype(BF)
    placed = jnp.dot(stacked, places, preferred_element_type=F32).astype(BF)
    for c in range(C):
        for group in range(groups):
            at = (c * groups + group) * local
            for t in range(T):
                out_ref[c * T + t, :, group * 128 : (group + 1) * 128] = placed[
                    at : at + local, t * 128 : (t + 1) * 128
                ]


def normed_parts(z, checkpoint, gain):
    local, width = checkpoint.shape
    return pl.pallas_call(
        normed_kernel,
        in_specs=[SMEM, VMEM, VMEM],
        out_specs=VMEM,
        out_shape=jax.ShapeDtypeStruct((C * T, local, width // (C * T)), BF),
        scratch_shapes=[pltpu.VMEM((local, width), BF)],
        compiler_params=params(20),
        cost_estimate=cost(2 * local * width * 1024, 4 * local * width),
    )(z.reshape(1), checkpoint, gain)


def terms_kernel(cot_ref, w_ref, *refs):
    outs, token = refs[-T - 1 : -1], refs[-1]
    token[...] = jnp.zeros(token.shape, F32)
    product = lax.dot_general(
        cot_ref[...], w_ref[...], (((1,), (1,)), ((), ())), preferred_element_type=F32
    )
    rows = product.shape[0] // T
    for i, out in enumerate(outs):
        out[...] = product[i * rows : (i + 1) * rows].astype(BF)


def grad_terms(cot, weight, *tokens, tile=2048):
    rows, depth = cot.shape
    width = weight.shape[0]
    own = rows // T
    outs = pl.pallas_call(
        terms_kernel,
        grid=(width // tile,),
        in_specs=[
            pl.BlockSpec((rows, depth), lambda i: (0, 0)),
            pl.BlockSpec((tile, depth), lambda i: (i, 0)),
        ]
        + [ANY] * len(tokens),
        out_specs=[pl.BlockSpec((own, tile), lambda i: (0, i))] * T
        + [pl.BlockSpec((8, 128), lambda i: (0, 0))],
        out_shape=[jax.ShapeDtypeStruct((own, width), BF)] * T
        + [jax.ShapeDtypeStruct((8, 128), F32)],
        compiler_params=params(58),
        cost_estimate=cost(
            4 * rows * depth * width, 2 * (rows * depth + width * depth + rows * width)
        ),
    )(cot, weight, *tokens)
    return outs[:T], outs[T]


def weight_kernel(scale, count, core_ref, left_ref, *refs):
    outs = refs[-Z - 1 : -1]
    turned = refs[-1]
    tokens = left_ref.shape[1]

    @pl.when(pl.program_id(0) == 0)
    def _():
        turned[:, :tokens] = left_ref[core_ref[0]].T
        turned[:, tokens:] = left_ref[1 - core_ref[0]].T

    for i in range(count):

        @pl.when(pl.program_id(0) == i)
        def _():
            right = jnp.concatenate([refs[i][...], refs[count + i][...]], axis=0)
            product = jnp.dot(turned[...], right, preferred_element_type=F32)
            product = (product * scale).astype(BF)
            rows = product.shape[0] // Z
            for k, out in enumerate(outs):
                out[...] = product[k * rows : (k + 1) * rows].reshape(out.shape)


def weight_terms(core, left, own, other, scale, *tokens):
    cores, rows, features = left.shape
    columns = own[0].shape[1]
    count = len(own)
    fine = features // (Z * H)
    whole = lambda shape: pl.BlockSpec(shape, lambda i: (0,) * len(shape))
    return pl.pallas_call(
        functools.partial(weight_kernel, scale, count),
        grid=(count,),
        in_specs=[SMEM, whole(left.shape)]
        + [whole(own[0].shape)] * (2 * count)
        + [ANY] * len(tokens),
        out_specs=[pl.BlockSpec((H, 1, fine, columns), lambda i: (0, i, 0, 0))] * Z,
        out_shape=[jax.ShapeDtypeStruct((H, count, fine, columns), BF)] * Z,
        scratch_shapes=[pltpu.VMEM((features, cores * rows), BF)],
        compiler_params=params(58),
        cost_estimate=cost(
            2 * features * cores * rows * columns * count,
            2 * (features * cores * rows + (cores * rows + features) * columns * count),
        ),
    )(core.reshape(1), left, *own, *other, *tokens)


def sums_kernel(sizes, *refs):
    outs = refs[-len(sizes) :]
    at = 0
    for size, out in zip(sizes, outs):
        out[...] = add(*[ref[...] for ref in refs[at : at + size]]).astype(BF)
        at += size


def sums(groups, *tokens, steps=1):
    values = [value for group in groups for value in group]
    shape = values[0].shape
    block = shape[:-1] + (shape[-1] // steps,)
    spec = pl.BlockSpec(block, lambda i: (0,) * (len(shape) - 1) + (i,))
    return pl.pallas_call(
        functools.partial(sums_kernel, [len(group) for group in groups]),
        grid=(steps,),
        in_specs=[spec] * len(values) + [ANY] * len(tokens),
        out_specs=[spec] * len(groups),
        out_shape=[jax.ShapeDtypeStruct(shape, BF) for group in groups],
        compiler_params=params(16),
        cost_estimate=cost(values[0].size * len(values), 2 * values[0].size * len(values)),
    )(*values, *tokens)


def input_kernel(check_ref, gain_ref, *refs):
    out_ref = refs[-1]
    values = check_ref[...].astype(F32)
    inv_rms = lax.rsqrt(jnp.mean(values * values, axis=1, keepdims=True) + 1e-05)
    unit_rows = values * inv_rms
    scaled = add(*[ref[...] for ref in refs[:4]]) * gain_ref[...].astype(F32)
    mean = jnp.mean(scaled * unit_rows, axis=1, keepdims=True)
    out_ref[...] = (inv_rms * (scaled - unit_rows * mean)).astype(BF)


def input_out(checkpoint, gain, parts, *tokens, rows=16):
    local, width = checkpoint.shape
    spec = pl.BlockSpec((rows, width), lambda i: (i, 0))
    return pl.pallas_call(
        input_kernel,
        grid=(local // rows,),
        in_specs=[spec, pl.BlockSpec((1, width), lambda i: (0, 0))]
        + [spec] * len(parts)
        + [ANY] * len(tokens),
        out_specs=spec,
        out_shape=jax.ShapeDtypeStruct((local, width), BF),
        compiler_params=params(24),
        cost_estimate=cost(12 * local * width, 12 * local * width),
    )(checkpoint, gain, *parts, *tokens)


def blocks_kernel(order_ref, weight_ref, *refs):
    out_ref = refs[-1]
    columns = weight_ref.shape[-1]
    fine = weight_ref.shape[2]
    count = T // 2
    dots = [jnp.zeros((fine, 1), F32) for _ in range(H)]
    for i in range(T):
        terms = refs[3 * (i // count) : 3 * (i // count) + 3]
        t = order_ref[i]
        for h in range(H):
            value = add(*[term[h, i % count] for term in terms]).astype(BF)
            out_ref[h * T + t, :, :columns] = value
            product = value.astype(F32) * weight_ref[t, h].astype(F32)
            dots[h] += jnp.sum(product, axis=1, keepdims=True)
    lane = lax.broadcasted_iota(jnp.int32, (fine, 128), 1)
    for h in range(H):
        high = dots[h].astype(BF).astype(F32)
        extra = jnp.where(lane == 0, high, jnp.where(lane == 1, dots[h] - high, 0.0)).astype(BF)
        for t in range(T):
            out_ref[h * T + t, :, columns:] = extra


def last_blocks(order, weight, terms, *tokens):
    fine, columns = weight.shape[2:]
    return pl.pallas_call(
        blocks_kernel,
        in_specs=[SMEM] + [VMEM] * (1 + len(terms)) + [ANY] * len(tokens),
        out_specs=VMEM,
        out_shape=jax.ShapeDtypeStruct((H * T, fine, columns + 128), BF),
        compiler_params=params(8),
        cost_estimate=cost(5 << 20, 5 << 20),
    )(order, weight, *terms, *tokens)


def finish_kernel(group_ref, gain_ref, blocks_ref, weight_ref, gain_out_ref):
    columns = weight_ref.shape[1]
    fine = blocks_ref.shape[1]
    lane = lax.broadcasted_iota(jnp.int32, (8, 128), 1)
    pick = jnp.where(lane < 2, 1.0, 0.0).astype(BF)
    dots = jnp.zeros((8, weight_ref.shape[0]), F32)
    for h in range(H):
        extra = blocks_ref[h * T : (h + 1) * T, :, columns:].reshape(T * fine, 128)
        dots += lax.dot_general(pick, extra, (((1,), (1,)), ((), ())), preferred_element_type=F32)
    gain_out_ref[...] = dots[:1] / gain_ref[pl.ds(group_ref[0], 1), :].astype(F32)
    for t in range(T):
        weight_ref[t * fine : (t + 1) * fine] = add(
            *[blocks_ref[h * T + t, :, :columns] for h in range(H)]
        )


def finish(group, gain, blocks):
    fine, width = blocks.shape[1:]
    rows = T * fine
    weight, gain_row = pl.pallas_call(
        finish_kernel,
        in_specs=[SMEM, VMEM, VMEM],
        out_specs=[VMEM, VMEM],
        out_shape=[
            jax.ShapeDtypeStruct((rows, width - 128), F32),
            jax.ShapeDtypeStruct((1, rows), F32),
        ],
        compiler_params=params(8),
        cost_estimate=cost(5 << 20, 5 << 20),
    )(group.reshape(1), gain.astype(F32).reshape(-1, rows), blocks)
    return weight, gain_row.reshape(rows)


def shards(checkpoint, gain, qkv_weight, qkv_cot):
    h, z, c = lax.axis_index("h"), lax.axis_index("z"), lax.axis_index("c")
    x, l = lax.axis_index("x"), lax.axis_index("l")
    local, width = checkpoint.shape
    tokens, columns = qkv_cot.shape
    grad_scale = 1.0 / math.sqrt(tokens * H * Z * C)
    fine = width // (H * Z * C * T)
    gain_row = gain.reshape(1, width)

    with jax.named_scope("normed_exchange"):
        parts = normed_parts(z, checkpoint, gain_row)
        left = lax.all_to_all(parts, ("c",) + TENSOR, 0, 0, tiled=True)
        left = left.reshape(C, tokens, Z * H * fine)

    near = {(0, 0): qkv_cot}
    with jax.named_scope("cot_gather"):
        near[0, 1] = swap(qkv_cot, "l")
        for step in (1, 3, 2):
            near[step, 0] = shift(qkv_cot, "x", -step)

    with jax.named_scope("weight_rows"):
        mine = qkv_weight.reshape(H, Z, C, T, fine, columns)
        mine = lax.dynamic_slice(mine, (0, z, c, 0, 0, 0), (H, 1, 1, T, fine, columns))
        mine = after(mine.reshape(H, T, fine, columns).swapaxes(0, 1), parts)

    with jax.named_scope("input_terms"):
        cot_near = relative(qkv_cot.reshape(X, L, local, columns), x, l)
        term, multiplied = grad_terms(cot_near.reshape(tokens, columns), qkv_weight, parts, mine)

    keys = (((0, 0), (0, 1), (1, 0), (3, 0)), ((2, 0), (1, 1), (3, 1), (2, 1)))
    across = {(0, 0): swap(qkv_cot, "c")}

    def product(some, *given):
        own, other = [near[key] for key in some], [across[key] for key in some]
        return weight_terms(c, left, own, other, grad_scale, *given)

    with jax.named_scope("cot_gather"):
        for key in ((0, 1), (1, 0), (3, 0), (2, 0)):
            near[key] = after(near[key], multiplied, left)
        near[3, 1] = shift(near[0, 1], "x", 1)
        near[1, 1] = shift(near[0, 1], "x", -1)
        near[2, 1] = swap(near[2, 0], "l")
        for key in keys[0][1:]:
            across[key] = swap(near[key], "c")
    with jax.named_scope("weight_terms"):
        a = product(keys[0], multiplied)
    with jax.named_scope("cot_gather"):
        for key in keys[1]:
            near[key] = after(near[key], a[0])
            across[key] = swap(near[key], "c")
    with jax.named_scope("weight_terms"):
        b = product(keys[1], a[0])

    with jax.named_scope("chains"):
        up = lambda value: shift(value, "z", 1)
        down = lambda value: shift(value, "z", -1)
        term = after(term, near[1, 1], near[3, 1])
        term = {(i // L, i % L): term[i] for i in range(T)}
        up_a, down_a = up(a[4]), down(a[5])
        far_up, far_down = shift(term[2, 0], "x", 1), shift(term[2, 1], "x", -1)
        up_1 = shift(term[1, 1], "x", 1)
        up_b, down_b = up(b[3]), down(b[4])
        s1 = sums([(a[3], up_a), (a[6], down_a)], b[0])
        up_a, down_a = up(s1[0]), down(s1[1])
        s2 = sums([(term[3, 1], far_down), (term[1, 0], far_up)], s1[0], steps=4)
        down_1, up_0 = shift(s2[0], "x", -1), shift(s2[1], "x", 1)
        down_0 = shift(after(term[3, 0], s2[0]), "x", -1)
        s3 = sums([(b[2], up_b), (b[5], down_b)], s2[0])
        up_b, down_b = up(s3[0]), down(s3[1])
        s4 = sums([(a[2], up_a), (a[7], down_a)], s3[0])
        up_a, down_a = up(s4[0]), down(s4[1])
        s5 = sums([(b[1], up_b), (b[6], down_b)], s4[0])
        up_b, down_b = up(s5[0]), down(s5[1])
        s7 = sums([(a[1], up_a)], s5[0])
        up_a = up(s7[0])
        s8 = sums([(b[7], down_b)], s7[0])
        down_b = down(s8[0])
        s6 = sums([(term[0, 1], up_1, down_1)], s8[0], steps=4)
        other_l = swap(s6[0], "l")

    with jax.named_scope("weight_rows"):
        mine = lax.all_to_all(after(mine, s3[0]), TENSOR, 0, 0, tiled=True)

    with jax.named_scope("input_out"):
        input_grad = input_out(checkpoint, gain_row, (term[0, 0], up_0, down_0, other_l), s8[0])

    with jax.named_scope("weight_out"):
        order = jnp.stack(
            [lax.rem(x + i, X) * L + lax.rem(l + j, L) for some in keys for i, j in some]
        )
        blocks = last_blocks(order, mine, (a[0], up_a, down_a, b[0], up_b, down_b))
        blocks = lax.all_to_all(blocks, ("h",) + TENSOR, 0, 0, tiled=True)
        weight_out, gain_out = finish((h * Z + z) * C + c, gain, blocks)
    return (input_grad, gain_out, weight_out)


def solution(mesh):
    fine_mesh = Mesh(mesh.devices.reshape(H, Z, C, X, L), DP + TENSOR)
    rows = P(DP + TENSOR, None)
    in_specs = (rows, P(), P(None, TENSOR), P(DP, TENSOR))
    out_specs = (rows, P(DP), P(DP, TENSOR))
    return jax.shard_map(
        shards, mesh=fine_mesh, in_specs=in_specs, out_specs=out_specs, check_vma=False
    )
```
